32 devices in a mesh: dp: 4 (over y, x), tensor: 8 (over z, core).
Axes of the slice: x: 2, y: 2, z: 4, core: 2. Of those that a mesh axis runs over, the one named last changes fastest.
Arguments:
- tokens: bfloat16 [2048, 3584], P(('dp', 'tensor')), may hold values from -6 to 6
- cotangent: bfloat16 [2048, 3584], P(('dp', 'tensor')), may hold values from -6 to 6
- gate_weight: bfloat16 [3584, 10240], P(None, 'tensor'), may hold values from -0.09375 to 0.09375
- up_weight: bfloat16 [3584, 10240], P(None, 'tensor'), may hold values from -0.09375 to 0.09375
- down_weight: bfloat16 [10240, 3584], P('tensor'), may hold values from -0.0625 to 0.0625
- adapter_first_factors: bfloat16 [3584, 128], replicated, may hold values from -0.09375 to 0.09375
- adapter_second_factors: bfloat16 [2, 64, 10240], P(None, None, 'tensor'), may hold values from -0.75 to 0.75
- down_factor_first: bfloat16 [64, 10240], P(None, 'tensor'), may hold values from -0.0625 to 0.0625
- down_factor_second: bfloat16 [64, 3584], replicated, may hold values from -0.75 to 0.75
Outputs:
- input_gradient: bfloat16 [2048, 3584], P(('dp', 'tensor'))
- adapter_first_gradient: float32 [3584, 128], replicated
- adapter_second_gradient: float32 [2, 64, 10240], P(None, None, 'tensor')
- down_first_gradient: float32 [64, 10240], P(None, 'tensor')
- down_second_gradient: float32 [64, 3584], replicated
The draws below stay inside these ranges and needn't reach their ends.
All inputs are finite; a program needn't handle non-finite values.
Results may differ from the reference program's by a relative error of at most 0.017.
Values may be sent and summed in bfloat16 or wider, within the bound.
A program may use at most 128 MiB of HBM per device.

```python
import math
import jax
import jax.numpy as jnp
from jax import lax

MODEL_WIDTH = 3584
HIDDEN_UNITS = 10240
ADAPTER_RANK = 64
TOKEN_COUNT = 2048
N_TENSOR = 8


def levels(own_key, shape, pieces, low, high):
    loudness = 1.0
    for position, parts in pieces:
        draws = jax.random.uniform(jax.random.fold_in(jax.random.fold_in(own_key, 6), position), (parts,), jnp.float32, low / len(pieces), high / len(pieces))
        loudness = loudness * jnp.repeat(jnp.exp(draws), shape[position] // parts).reshape((-1,) + (1,) * (len(shape) - 1 - position))
    return loudness


def gaussian(rng, dims, spread, most, cuts=(), dtype=jnp.bfloat16):
    array = spread * jax.random.normal(rng, dims, jnp.float32)
    if cuts:
        array = array * levels(rng, dims, cuts, -0.22, 0.18)
    return jnp.clip(array, -most, most).astype(dtype)


def setup_inputs(seed: int = 0) -> dict:
    key_of = jax.random.split(jax.random.key(seed), 10)
    tokens = gaussian(key_of[0], (TOKEN_COUNT, MODEL_WIDTH), 1.0, 6.0, ((0, 32),))
    cotangent = gaussian(key_of[1], (TOKEN_COUNT, MODEL_WIDTH), 1.0, 6.0, ((0, 32),))
    gate_weight = gaussian(key_of[2], (MODEL_WIDTH, HIDDEN_UNITS), MODEL_WIDTH ** -0.5, 0.09375, ((1, 8),))
    up_weight = gaussian(key_of[3], (MODEL_WIDTH, HIDDEN_UNITS), MODEL_WIDTH ** -0.5, 0.09375, ((1, 8),))
    down_weight = gaussian(key_of[4], (HIDDEN_UNITS, MODEL_WIDTH), HIDDEN_UNITS ** -0.5, 0.0625, ((0, 8),))
    adapter_first_factors = gaussian(key_of[5], (MODEL_WIDTH, 2 * ADAPTER_RANK), MODEL_WIDTH ** -0.5, 0.09375)
    adapter_second_factors = gaussian(key_of[6], (2, ADAPTER_RANK, HIDDEN_UNITS), ADAPTER_RANK ** -0.5, 0.75, ((2, 8),))
    down_factor_first = gaussian(key_of[7], (ADAPTER_RANK, HIDDEN_UNITS), HIDDEN_UNITS ** -0.5, 0.0625, ((1, 8),))
    down_factor_second = gaussian(key_of[8], (ADAPTER_RANK, MODEL_WIDTH), ADAPTER_RANK ** -0.5, 0.75)
    return dict(tokens=tokens, cotangent=cotangent, gate_weight=gate_weight, up_weight=up_weight, down_weight=down_weight, adapter_first_factors=adapter_first_factors, adapter_second_factors=adapter_second_factors, down_factor_first=down_factor_first, down_factor_second=down_factor_second)


adapter_scale = 0.5

def contraction_rows(left, right):
    return lax.dot_general(left, right, (((0,), (0,)), ((), ())), preferred_element_type=jnp.float32)

def contract_columns(left, right):
    return lax.dot_general(left, right, (((1,), (1,)), ((), ())), preferred_element_type=jnp.float32)

def exact_rows(left, right):
    return lax.dot_general(left.astype(jnp.float32), right.astype(jnp.float32), (((0,), (0,)), ((), ())), precision=lax.Precision.HIGHEST, preferred_element_type=jnp.float32)

def exact_columns(left, right):
    return lax.dot_general(left.astype(jnp.float32), right.astype(jnp.float32), (((1,), (1,)), ((), ())), precision=lax.Precision.HIGHEST, preferred_element_type=jnp.float32)

def reference(tokens, cotangent, gate_weight, up_weight, down_weight, adapter_first_factors, adapter_second_factors, down_factor_first, down_factor_second):
    input_lowrank = jnp.dot(tokens, adapter_first_factors, preferred_element_type=jnp.float32).astype(jnp.bfloat16)
    gate_preactivation = jnp.dot(tokens, gate_weight, preferred_element_type=jnp.float32) + adapter_scale * jnp.dot(input_lowrank[:, :ADAPTER_RANK], adapter_second_factors[0], preferred_element_type=jnp.float32)
    up_preactivation = jnp.dot(tokens, up_weight, preferred_element_type=jnp.float32) + adapter_scale * jnp.dot(input_lowrank[:, ADAPTER_RANK:], adapter_second_factors[1], preferred_element_type=jnp.float32)
    sigmoid = jax.nn.sigmoid(gate_preactivation)
    active = gate_preactivation * sigmoid
    hidden = (active * up_preactivation).astype(jnp.bfloat16)
    hid_low = contract_columns(hidden, down_factor_first)
    output_gradient_lowrank = contract_columns(cotangent, down_factor_second).astype(jnp.bfloat16)
    hidden_gradient = contract_columns(cotangent, down_weight) + adapter_scale * jnp.dot(output_gradient_lowrank, down_factor_first, preferred_element_type=jnp.float32)
    gate_gradient = (hidden_gradient * up_preactivation * sigmoid * (1.0 + gate_preactivation * (1.0 - sigmoid))).astype(jnp.bfloat16)
    up_gradient = (hidden_gradient * active).astype(jnp.bfloat16)
    lowrank_projected = jnp.concatenate([contract_columns(gate_gradient, adapter_second_factors[0]), contract_columns(up_gradient, adapter_second_factors[1])], axis=1)
    span_width = HIDDEN_UNITS // N_TENSOR

    def add_block(block, total):
        offset = (block * span_width).astype(jnp.int32)
        gate_part = lax.dynamic_slice_in_dim(gate_gradient, offset, span_width, 1)
        up_part = lax.dynamic_slice_in_dim(up_gradient, offset, span_width, 1)
        wg_part = lax.dynamic_slice_in_dim(gate_weight, offset, span_width, 1)
        wu_part = lax.dynamic_slice_in_dim(up_weight, offset, span_width, 1)
        term = contract_columns(gate_part, wg_part) + contract_columns(up_part, wu_part)
        rounded = lax.optimization_barrier(term.astype(jnp.bfloat16))
        return total + rounded.astype(jnp.float32)
    frozen_matrix = lax.fori_loop(0, N_TENSOR, add_block, jnp.zeros((tokens.shape[0], MODEL_WIDTH), jnp.float32))
    input_gradient = (frozen_matrix + adapter_scale * exact_columns(lowrank_projected, adapter_first_factors)).astype(jnp.bfloat16)
    factor_matrix = adapter_scale / math.sqrt(TOKEN_COUNT)
    adapter_first_gradient = factor_matrix * exact_rows(tokens, lowrank_projected)
    adapter_second_gradient = factor_matrix * jnp.stack([contraction_rows(input_lowrank[:, :ADAPTER_RANK], gate_gradient), contraction_rows(input_lowrank[:, ADAPTER_RANK:], up_gradient)])
    down_first_gradient = factor_matrix * contraction_rows(output_gradient_lowrank, hidden)
    down_second_gradient = factor_matrix * exact_rows(hid_low, cotangent)
    return (input_gradient, adapter_first_gradient, adapter_second_gradient, down_first_gradient, down_second_gradient)
```

```python
import functools
import math

import jax
import jax.numpy as jnp
from jax import lax
from jax.experimental import pallas as pl
from jax.experimental.pallas import tpu as pltpu
from jax.sharding import PartitionSpec as P

adapter_scale = 0.5
bf16 = jnp.bfloat16
f32 = jnp.float32
MESH = pl.DeviceIdType.MESH


def dot(a, b):
    return jnp.dot(a, b, preferred_element_type=f32)


def dot_nt(a, b):
    return lax.dot_general(a, b, (((1,), (1,)), ((), ())), preferred_element_type=f32)


def kernel(
    n, m, T, H, R, TW, W, CW,
    x_ref, dy_ref, wg_ref, wu_ref, wd_ref, a1_ref, a2_ref, df_ref, d2_ref,
    ig_ref, g_ref, p_ref,
    xg, dyg, wg, wu, wd, gate, up, dgate, dup, hid,
    xlow, xlow_t, dylow, dylow_t, low, lowb, lowr, ulow, u_own,
    pb, precv, term, die, rsr, piece, piecer, gbuf,
    load_sem, x_s, x_r, dy_s, dy_r, low_s, low_r, ul_s, ul_r,
    p_s, p_r, die_s, die_r, rs_s, rs_r, pc_s, pc_r, g_s, g_r,
):
    t = lax.axis_index("tensor")
    d = lax.axis_index("dp")
    nz = n // 2
    core = lax.rem(t, 2)
    z = lax.div(t, 2)
    G = n * T
    D = x_ref.shape[1]
    NC = D // W
    NT = H // TW
    nch = D // CW

    def rows(b):
        return pl.ds(pl.multiple_of(b * T, T), T)

    loads = [
        pltpu.make_async_copy(src, dst, load_sem.at[i])
        for i, (src, dst) in enumerate(
            [(x_ref, xg.at[rows(t)]), (dy_ref, dyg.at[rows(t)]), (wg_ref, wg), (wu_ref, wu), (wd_ref, wd)]
        )
    ]
    for c in loads:
        c.start()

    barrier = pltpu.get_barrier_semaphore()
    for k in range(1, n):
        pl.semaphore_signal(barrier, inc=1, device_id={"tensor": lax.rem(t + k, n)}, device_id_type=MESH)
    for k in range(1, m):
        pl.semaphore_signal(barrier, inc=1, device_id={"dp": lax.rem(d + k, m)}, device_id_type=MESH)
    pl.semaphore_wait(barrier, n - 1 + m - 1)

    right = lax.rem(t + 1, n)
    left = lax.rem(t + n - 1, n)

    def hop(at, s_sem, r_sem, side, b):
        return pltpu.make_async_remote_copy(
            src_ref=at(b), dst_ref=at(b), send_sem=s_sem.at[side, b], recv_sem=r_sem.at[b],
            device_id={"tensor": right if side == 0 else left}, device_id_type=MESH,
        )

    def forward(at, s_sem, r_sem, s, limit, first):
        b = t - s

        @pl.when(jnp.logical_and(b >= 0, b < limit))
        def _():
            if not first:
                hop(at, s_sem, r_sem, 0, b).wait_recv()

            @pl.when(t < n - 1)
            def _():
                hop(at, s_sem, r_sem, 0, b).start()

        b2 = t + s

        @pl.when(b2 < limit)
        def _():
            if not first:
                hop(at, s_sem, r_sem, 1, b2).wait_recv()

            @pl.when(t > 0)
            def _():
                hop(at, s_sem, r_sem, 1, b2).start()

    def drain(at, s_sem, r_sem, limit):
        def body(b, carry):
            @pl.when(jnp.logical_and(b <= t, t < n - 1))
            def _():
                hop(at, s_sem, r_sem, 0, b).wait_send()

            @pl.when(jnp.logical_and(b >= t, t > 0))
            def _():
                hop(at, s_sem, r_sem, 1, b).wait_send()

            return carry

        lax.fori_loop(0, limit, body, 0)

    def x_at(b):
        return xg.at[rows(b)]

    def dy_at(b):
        return dyg.at[rows(b)]

    def g_at(b):
        return gbuf.at[b]

    def loop(lo, hi, body):
        def step(i, carry):
            body(i)
            return carry

        lax.fori_loop(lo, hi, step, 0)

    loads[0].wait()
    loads[1].wait()
    forward(x_at, x_s, x_r, 0, n, True)
    loop(1, n, lambda s: forward(x_at, x_s, x_r, s, n, False))

    forward(dy_at, dy_s, dy_r, 0, n, True)
    xl = dot(xg[...], a1_ref[...])
    xlow[...] = xl.astype(bf16)
    xlow_t[...] = xl.T.astype(bf16)
    loads[2].wait()
    loads[3].wait()

    def forward_tile(j):
        cols = pl.ds(pl.multiple_of(j * TW, TW), TW)
        gate[:, cols] = dot(xg[...], wg[:, cols]) + adapter_scale * dot(xlow[:, :R], a2_ref[0, :, cols])
        up[:, cols] = dot(xg[...], wu[:, cols]) + adapter_scale * dot(xlow[:, R:], a2_ref[1, :, cols])

    def dy_step(s):
        forward(dy_at, dy_s, dy_r, s, n, False)

        @pl.when(s - 1 < NT)
        def _():
            forward_tile(s - 1)

    loop(1, n, dy_step)
    if NT > n - 1:
        loop(n - 1, NT, forward_tile)

    loads[4].wait()
    dl = dot_nt(dyg[...], d2_ref[...])
    dylow[...] = dl.astype(bf16)
    dylow_t[...] = dl.T.astype(bf16)
    low[...] = jnp.zeros_like(low)

    def backward_tile(j):
        cols = pl.ds(pl.multiple_of(j * TW, TW), TW)
        dh = dot_nt(dyg[...], wd[cols, :]) + adapter_scale * dot(dylow[...], df_ref[:, cols])
        gp = gate[:, cols]
        u = up[:, cols]
        sig = jax.nn.sigmoid(gp)
        act = gp * sig
        dg = (dh * u * sig * (1.0 + gp * (1.0 - sig))).astype(bf16)
        du = (dh * act).astype(bf16)
        hd = (act * u).astype(bf16)
        dgate[:, cols] = dg
        dup[:, cols] = du
        pb[:R, cols] = dot(xlow_t[:R, :], dg).astype(bf16)
        pb[R : 2 * R, cols] = dot(xlow_t[R:, :], du).astype(bf16)
        pb[2 * R :, cols] = dot(dylow_t[...], hd).astype(bf16)
        low[:, :R] += dot_nt(dg, a2_ref[0, :, cols])
        low[:, R : 2 * R] += dot_nt(du, a2_ref[1, :, cols])
        low[:, 2 * R :] += dot_nt(hd, df_ref[:, cols])

    loop(0, NT, backward_tile)

    lowb[...] = low[...].astype(bf16)

    def low_copy(k):
        peer = lax.rem(t + k, n)
        return pltpu.make_async_remote_copy(
            src_ref=lowb.at[rows(peer)], dst_ref=lowr.at[t], send_sem=low_s.at[k], recv_sem=low_r.at[t],
            device_id={"tensor": peer}, device_id_type=MESH,
        )

    def low_arrival(k):
        peer = lax.rem(t + k, n)
        return pltpu.make_async_remote_copy(
            src_ref=lowb.at[rows(peer)], dst_ref=lowr.at[peer], send_sem=low_s.at[k], recv_sem=low_r.at[peer],
            device_id={"tensor": peer}, device_id_type=MESH,
        )

    def ul_copy(k, b):
        peer = lax.rem(t + k, n)
        return pltpu.make_async_remote_copy(
            src_ref=ulow.at[rows(b)], dst_ref=ulow.at[rows(b)], send_sem=ul_s.at[k], recv_sem=ul_r.at[b],
            device_id={"tensor": peer}, device_id_type=MESH,
        )

    def dp_copy(src, dst, s_sem, r_sem, k, slot):
        peer = lax.rem(d + k, m)
        return pltpu.make_async_remote_copy(
            src_ref=src, dst_ref=dst.at[slot], send_sem=s_sem.at[k], recv_sem=r_sem.at[slot],
            device_id={"dp": peer}, device_id_type=MESH,
        )

    loop(1, n, lambda k: low_copy(k).start())
    loop(1, m, lambda k: dp_copy(pb, precv, p_s, p_r, k, d).start())

    partner = t + 1 - 2 * core

    def die_copy(c):
        return pltpu.make_async_remote_copy(
            src_ref=term.at[c, 1 - core], dst_ref=die.at[c], send_sem=die_s.at[c], recv_sem=die_r.at[c],
            device_id={"tensor": partner}, device_id_type=MESH,
        )

    def rs_copy(c, k, slot):
        other = lax.rem(z + k, nz)
        return pltpu.make_async_remote_copy(
            src_ref=term.at[c, core, other], dst_ref=rsr.at[c, slot], send_sem=rs_s.at[c, k],
            recv_sem=rs_r.at[c, slot], device_id={"tensor": 2 * other + core}, device_id_type=MESH,
        )

    def chip_sum(c):
        die_copy(c).wait_recv()
        term[c, core] = (term[c, core].astype(f32) + die[c].astype(f32)).astype(bf16)
        for k in range(1, nz):
            rs_copy(c, k, z).start()

    def term_tile(c):
        span = pl.ds(pl.multiple_of(c * W, W), W)
        v = (dot_nt(dgate[...], wg[span, :]) + dot_nt(dup[...], wu[span, :])).astype(bf16)
        v = v.reshape(nz, 2, T, W)
        term[c, 0] = v[:, 0]
        term[c, 1] = v[:, 1]
        die_copy(c).start()

        @pl.when(c > 0)
        def _():
            chip_sum(c - 1)

    cut1, cut2, cut3 = NC // 4, NC // 2, (3 * NC) // 4
    loop(0, cut1, term_tile)

    lowr[t] = lowb[rows(t), :]
    loop(1, n, lambda k: low_arrival(k).wait_recv())
    total = lowr[0].astype(f32)
    for b in range(1, n):
        total = total + lowr[b].astype(f32)
    u_own[...] = total.astype(bf16)
    ulow[rows(t), :] = total.astype(bf16)
    loop(1, n, lambda k: ul_copy(k, t).start())

    loop(cut1, cut2, term_tile)

    loop(1, n, lambda k: ul_copy(k, lax.rem(t + k, n)).wait_recv())

    @pl.when(t < nch)
    def _():
        cols = pl.ds(pl.multiple_of(t * CW, CW), CW)
        u_t = ulow[...].astype(f32).T.astype(bf16)
        piece[: 2 * R, :] = dot(u_t[: 2 * R], xg[:, cols]).astype(bf16)
        piece[2 * R :, :] = dot(u_t[2 * R :], dyg[:, cols]).astype(bf16)
        loop(1, m, lambda k: dp_copy(piece, piecer, pc_s, pc_r, k, d).start())

    loop(cut2, cut3, term_tile)

    @pl.when(t < nch)
    def _():
        piecer[d] = piece[...]
        loop(1, m, lambda k: dp_copy(piece, piecer, pc_s, pc_r, k, lax.rem(d + k, m)).wait_recv())
        acc = piecer[0].astype(f32)
        for e in range(1, m):
            acc = acc + piecer[e].astype(f32)
        gbuf[t] = acc.astype(bf16)
        forward(g_at, g_s, g_r, 0, nch, True)

    loop(cut3, NC, term_tile)
    chip_sum(NC - 1)

    precv[d] = pb[...]
    loop(1, m, lambda k: dp_copy(pb, precv, p_s, p_r, k, lax.rem(d + k, m)).wait_recv())
    acc = precv[0].astype(f32)
    for e in range(1, m):
        acc = acc + precv[e].astype(f32)
    p_ref[...] = acc

    loop(1, n, lambda s: forward(g_at, g_s, g_r, s, nch, False))
    g_ref[...] = gbuf[...]

    def finish(c):
        span = pl.ds(pl.multiple_of(c * W, W), W)
        total = term[c, core, z].astype(f32) + adapter_scale * dot_nt(u_own[:, : 2 * R], a1_ref[span, :])
        for k in range(1, nz):
            other = lax.rem(z + k, nz)
            rs_copy(c, k, other).wait_recv()
            total = total + rsr[c, other].astype(f32)
        ig_ref[:, span] = total.astype(bf16)

    loop(0, NC, finish)

    drain(x_at, x_s, x_r, n)
    drain(dy_at, dy_s, dy_r, n)
    drain(g_at, g_s, g_r, nch)
    loop(1, n, lambda k: low_copy(k).wait_send())
    loop(1, n, lambda k: ul_copy(k, t).wait_send())
    loop(1, m, lambda k: dp_copy(pb, precv, p_s, p_r, k, d).wait_send())

    @pl.when(t < nch)
    def _():
        loop(1, m, lambda k: dp_copy(piece, piecer, pc_s, pc_r, k, d).wait_send())

    def sent(c):
        die_copy(c).wait_send()
        for k in range(1, nz):
            rs_copy(c, k, z).wait_send()

    loop(0, NC, sent)


def shards(x, dy, wg, wu, wd, a1, a2, df, d2):
    n = lax.axis_size("tensor")
    m = lax.axis_size("dp")
    T, D = x.shape
    H = wg.shape[1]
    R = a2.shape[1]
    G = n * T
    TW = 256 if H % 256 == 0 else 128
    W = 256
    NC = D // W
    CW = -(-D // (n * 128)) * 128
    nch = D // CW
    factor = adapter_scale / math.sqrt(T * n * m)
    nz = n // 2
    V = pltpu.VMEM
    DMA = pltpu.SemaphoreType.DMA
    any_spec = pl.BlockSpec(memory_space=pl.ANY)
    vmem_spec = pl.BlockSpec(memory_space=pltpu.VMEM)
    macs = 5 * G * D * H
    ig, g, p = pl.pallas_call(
        functools.partial(kernel, n, m, T, H, R, TW, W, CW),
        out_shape=(
            jax.ShapeDtypeStruct((T, D), bf16),
            jax.ShapeDtypeStruct((nch, 3 * R, CW), bf16),
            jax.ShapeDtypeStruct((3 * R, H), f32),
        ),
        in_specs=[any_spec] * 5 + [vmem_spec] * 4,
        out_specs=(vmem_spec,) * 3,
        scratch_shapes=[
            V((G, D), bf16), V((G, D), bf16),
            V((D, H), bf16), V((D, H), bf16), V((H, D), bf16),
            V((G, H), f32), V((G, H), f32),
            V((G, H), bf16), V((G, H), bf16), V((8, 128), bf16),
            V((G, 2 * R), bf16), V((2 * R, G), bf16), V((G, R), bf16), V((R, G), bf16),
            V((G, 3 * R), f32), V((G, 3 * R), bf16), V((n, T, 3 * R), bf16),
            V((G, 3 * R), bf16), V((T, 3 * R), bf16),
            V((3 * R, H), bf16), V((m, 3 * R, H), bf16),
            V((NC, 2, nz, T, W), bf16), V((NC, nz, T, W), bf16), V((NC, nz, T, W), bf16),
            V((3 * R, CW), bf16), V((m, 3 * R, CW), bf16), V((nch, 3 * R, CW), bf16),
            DMA((5,)),
            DMA((2, n)), DMA((n,)), DMA((2, n)), DMA((n,)),
            DMA((n,)), DMA((n,)), DMA((n,)), DMA((n,)),
            DMA((m,)), DMA((m,)),
            DMA((NC,)), DMA((NC,)), DMA((NC, nz)), DMA((NC, nz)),
            DMA((m,)), DMA((m,)), DMA((2, n)), DMA((n,)),
        ],
        compiler_params=pltpu.CompilerParams(
            collective_id=0, has_side_effects=True, vmem_limit_bytes=63 * 1024 * 1024
        ),
        cost_estimate=pl.CostEstimate(flops=2 * macs, bytes_accessed=6 * D * H, transcendentals=G * H),
    )(x, dy, wg, wu, wd, a1, a2, df, d2)
    g = factor * g.astype(f32)
    first = g[:, : 2 * R].transpose(0, 2, 1).reshape(D, 2 * R)
    second = g[:, 2 * R :].transpose(1, 0, 2).reshape(R, D)
    p = factor * p
    return ig, first, p[: 2 * R].reshape(2, R, H), p[2 * R :], second


def solution(mesh):
    in_specs = (
        P(("dp", "tensor"), None),
        P(("dp", "tensor"), None),
        P(None, "tensor"),
        P(None, "tensor"),
        P("tensor", None),
        P(),
        P(None, None, "tensor"),
        P(None, "tensor"),
        P(),
    )
    out_specs = (P(("dp", "tensor"), None), P(), P(None, None, "tensor"), P(None, "tensor"), P())
    return jax.shard_map(shards, mesh=mesh, in_specs=in_specs, out_specs=out_specs, check_vma=False)
```

```python
import functools
import math

import jax
import jax.numpy as jnp
from jax import lax
from jax.experimental import pallas as pl
from jax.experimental.pallas import tpu as pltpu
from jax.sharding import PartitionSpec as P

adapter_scale = 0.5
bf16 = jnp.bfloat16
f32 = jnp.float32
MESH = pl.DeviceIdType.MESH


def dot(a, b):
    return jnp.dot(a, b, preferred_element_type=f32)


def dot_nt(a, b):
    return lax.dot_general(a, b, (((1,), (1,)), ((), ())), preferred_element_type=f32)


def kernel(
    n, m, T, H, R, TW, W, cp, cg,
    x_ref, dy_ref, wg_ref, wu_ref, wd_ref, a1_ref, a2_ref, df_ref, d2_ref,
    ig_ref, first_ref, second_ref, p2_ref, p1_ref,
    xg, dyg, wg, wu, wd, gate, up, dgate, dup,
    xlow, xlow_t, dylow, dylow_t, low, lowb, lowr, ulow, u_own,
    pacc, psend, precv, pfin, gsend, grecv, gfin, term, die, rsr,
    load_sem, x_s, x_r, dy_s, dy_r, low_s, low_r, ul_s, ul_r,
    p_s, p_r, pf_s, pf_r, g_s, g_r, gf_s, gf_r, gd_s, gd_r, die_s, die_r, rs_s, rs_r,
):
    t = lax.axis_index("tensor")
    d = lax.axis_index("dp")
    nz = n // 2
    core = lax.rem(t, 2)
    z = lax.div(t, 2)
    partner = t + 1 - 2 * core
    S = T // 2
    D = x_ref.shape[1]
    NC = D // W
    NT = H // TW
    HC = H // 128
    DC = D // 128

    def rows(b):
        return pl.ds(pl.multiple_of(b * S, S), S)

    def loop(lo, hi, body):
        def step(i, carry):
            body(i)
            return carry

        lax.fori_loop(lo, hi, step, 0)

    pairs = []
    for h in range(2):
        part = pl.ds(h * S, S)
        pairs += [(x_ref.at[part], xg.at[h, rows(t)]), (dy_ref.at[part], dyg.at[h, rows(t)])]
    pairs += [(wg_ref, wg), (wu_ref, wu), (wd_ref, wd)]
    loads = [pltpu.make_async_copy(src, dst, load_sem.at[i]) for i, (src, dst) in enumerate(pairs)]
    for c in loads:
        c.start()

    barrier = pltpu.get_barrier_semaphore()
    for k in range(1, n):
        pl.semaphore_signal(barrier, inc=1, device_id={"tensor": lax.rem(t + k, n)}, device_id_type=MESH)
    for k in range(1, m):
        pl.semaphore_signal(barrier, inc=1, device_id={"dp": lax.rem(d + k, m)}, device_id_type=MESH)
    pl.semaphore_wait(barrier, n - 1 + m - 1)

    right = lax.rem(t + 1, n)
    left = lax.rem(t + n - 1, n)

    def hop(line, side, b):
        buf, s_sem, r_sem, h = line
        return pltpu.make_async_remote_copy(
            src_ref=buf.at[h, rows(b)], dst_ref=buf.at[h, rows(b)], send_sem=s_sem.at[h, side, b],
            recv_sem=r_sem.at[h, b], device_id={"tensor": right if side == 0 else left}, device_id_type=MESH,
        )

    def forward(line, s, first=False):
        b = t - s

        @pl.when(b >= 0)
        def _():
            if not first:
                hop(line, 0, b).wait_recv()

            @pl.when(t < n - 1)
            def _():
                hop(line, 0, b).start()

        b2 = t + s

        @pl.when(b2 < n)
        def _():
            if not first:
                hop(line, 1, b2).wait_recv()

            @pl.when(t > 0)
            def _():
                hop(line, 1, b2).start()

    def drain(line):
        def body(b):
            @pl.when(jnp.logical_and(b <= t, t < n - 1))
            def _():
                hop(line, 0, b).wait_send()

            @pl.when(jnp.logical_and(b >= t, t > 0))
            def _():
                hop(line, 1, b).wait_send()

        loop(0, n, body)

    lines_x = [(xg, x_s, x_r, h) for h in range(2)]
    lines_dy = [(dyg, dy_s, dy_r, h) for h in range(2)]

    def tile_cols(j):
        return pl.ds(pl.multiple_of(j * TW, TW), TW)

    def input_rank(h):
        xl = dot(xg[h], a1_ref[...])
        xlow[...] = xl.astype(bf16)
        xlow_t[...] = xl.T.astype(bf16)

    def forward_tile(h, j):
        cols = tile_cols(j)
        gate[:, cols] = dot(xg[h], wg[:, cols]) + adapter_scale * dot(xlow[:, :R], a2_ref[0, :, cols])
        up[:, cols] = dot(xg[h], wu[:, cols]) + adapter_scale * dot(xlow[:, R:], a2_ref[1, :, cols])

    def cotangent_rank(h):
        dl = dot_nt(dyg[h], d2_ref[...])
        dylow[...] = dl.astype(bf16)
        dylow_t[...] = dl.T.astype(bf16)
        low[...] = jnp.zeros_like(low)

    def backward_tile(h, j):
        cols = tile_cols(j)
        dh = dot_nt(dyg[h], wd[cols, :]) + adapter_scale * dot(dylow[...], df_ref[:, cols])
        gp = gate[:, cols]
        u = up[:, cols]
        sig = jax.nn.sigmoid(gp)
        act = gp * sig
        dg = (dh * u * sig * (1.0 + gp * (1.0 - sig))).astype(bf16)
        du = (dh * act).astype(bf16)
        hd = (act * u).astype(bf16)
        dgate[:, cols] = dg
        dup[:, cols] = du
        for i, (a, b) in enumerate([(xlow_t[:R, :], dg), (xlow_t[R:, :], du), (dylow_t[...], hd)]):
            v = dot(a, b)
            if h == 0:
                pacc[i, :, cols] = v
            else:
                pacc[i, :, cols] += v
        low[:, :R] += dot_nt(dg, a2_ref[0, :, cols])
        low[:, R : 2 * R] += dot_nt(du, a2_ref[1, :, cols])
        low[:, 2 * R :] += dot_nt(hd, df_ref[:, cols])

    def keep_low(h):
        lowb[:, h] = low[...].astype(bf16).reshape(n, S, 3 * R)

    def send_to(src, dst, s_sem, r_sem, peer):
        return pltpu.make_async_remote_copy(
            src_ref=src, dst_ref=dst, send_sem=s_sem, recv_sem=r_sem, device_id=peer, device_id_type=MESH
        )

    def low_copy(k, slot):
        peer = lax.rem(t + k, n)
        return send_to(lowb.at[peer], lowr.at[slot], low_s.at[k], low_r.at[slot], {"tensor": peer})

    def ul_copy(k, slot):
        peer = lax.rem(t + k, n)
        return send_to(ulow.at[slot], ulow.at[slot], ul_s.at[k], ul_r.at[slot], {"tensor": peer})

    def scatter_copy(src, dst, s_sem, r_sem, k, slot):
        peer = lax.rem(d + k, m)
        return send_to(src.at[peer], dst.at[slot], s_sem.at[k], r_sem.at[slot], {"dp": peer})

    def p_copy(k, slot):
        return scatter_copy(psend, precv, p_s, p_r, k, slot)

    def g_copy(k, slot):
        return scatter_copy(gsend, grecv, g_s, g_r, k, slot)

    def pf_copy(k, slot):
        peer = lax.rem(d + k, m)
        return send_to(pfin.at[slot], pfin.at[slot], pf_s.at[k], pf_r.at[slot], {"dp": peer})

    def gf_copy(k, slot):
        peer = lax.rem(d + k, m)
        at = gfin.at[core, slot]
        return send_to(at, at, gf_s.at[k], gf_r.at[slot], {"dp": peer})

    def gd_copy(side, slot):
        at = gfin.at[side, slot]
        return send_to(at, at, gd_s.at[slot], gd_r.at[slot], {"tensor": partner})

    def other_d(k):
        return lax.rem(d + k, m)

    def die_copy(h, c):
        return send_to(term.at[h, c, 1 - core], die.at[h, c], die_s.at[h, c], die_r.at[h, c], {"tensor": partner})

    def rs_copy(h, c, k, slot):
        other = lax.rem(z + k, nz)
        return send_to(
            term.at[h, c, core, other], rsr.at[h, c, slot], rs_s.at[h, c, k], rs_r.at[h, c, slot],
            {"tensor": 2 * other + core},
        )

    def chip_sum(h, c):
        die_copy(h, c).wait_recv()
        term[h, c, core] = (term[h, c, core].astype(f32) + die[h, c].astype(f32)).astype(bf16)
        for k in range(1, nz):
            rs_copy(h, c, k, z).start()

    def term_tile(h, c):
        span = pl.ds(pl.multiple_of(c * W, W), W)
        v = (dot_nt(dgate[...], wg[span, :]) + dot_nt(dup[...], wu[span, :])).astype(bf16)
        v = v.reshape(nz, 2, S, W)
        term[h, c, 0] = v[:, 0]
        term[h, c, 1] = v[:, 1]
        die_copy(h, c).start()

        @pl.when(c > 0)
        def _():
            chip_sum(h, c - 1)

    loads[0].wait()
    forward(lines_x[0], 0, True)
    loop(1, n, lambda s: forward(lines_x[0], s))
    loads[1].wait()
    forward(lines_dy[0], 0, True)
    input_rank(0)
    loads[4].wait()
    loads[5].wait()

    def beside(line, s, h, tile):
        forward(line, s)

        @pl.when(s - 1 < NT)
        def _():
            tile(h, s - 1)

    loop(1, n, lambda s: beside(lines_dy[0], s, 0, forward_tile))
    loop(n - 1, NT, lambda j: forward_tile(0, j))

    loads[2].wait()
    forward(lines_x[1], 0, True)
    cotangent_rank(0)
    loads[6].wait()
    loop(1, n, lambda s: beside(lines_x[1], s, 0, backward_tile))
    loop(n - 1, NT, lambda j: backward_tile(0, j))

    loads[3].wait()
    forward(lines_dy[1], 0, True)
    keep_low(0)
    input_rank(1)
    per = -(-NC // (n - 1))

    def mixed(s):
        forward(lines_dy[1], s)
        for i in range(per):
            c = (s - 1) * per + i

            @pl.when(c < NC)
            def _():
                term_tile(0, c)

        @pl.when(s - 1 < NT)
        def _():
            forward_tile(1, s - 1)

    loop(1, n, mixed)
    loop(n - 1, NT, lambda j: forward_tile(1, j))
    chip_sum(0, NC - 1)

    cotangent_rank(1)
    loop(0, NT, lambda j: backward_tile(1, j))
    keep_low(1)

    loop(1, n, lambda k: low_copy(k, t).start())
    for q in range(m * cp):
        g, j = divmod(q, HC)
        if g < 3:
            psend[q // cp, q % cp] = pacc[g, :, 128 * j : 128 * (j + 1)].astype(bf16)
        else:
            psend[q // cp, q % cp] = jnp.zeros((R, 128), bf16)
    loop(1, m, lambda k: p_copy(k, d).start())

    cut1, cut2, cut3 = NC // 4, NC // 2, (3 * NC) // 4
    loop(0, cut1, lambda c: term_tile(1, c))

    lowr[t] = lowb[t]
    loop(1, n, lambda k: low_copy(k, lax.rem(t + k, n)).wait_recv())
    total = lowr[0].astype(f32)
    for b in range(1, n):
        total = total + lowr[b].astype(f32)
    u_own[...] = total.astype(bf16).reshape(T, 3 * R)
    ulow[t] = total.astype(bf16)
    loop(1, n, lambda k: ul_copy(k, t).start())

    loop(cut1, cut2, lambda c: term_tile(1, c))

    loop(1, n, lambda k: ul_copy(k, lax.rem(t + k, n)).wait_recv())
    u_t = [ulow[:, h].reshape(n * S, 3 * R).astype(f32).T.astype(bf16) for h in range(2)]
    for q in range(2 * m * cg):
        g, j = divmod(q, DC)
        if q % (m * cg) == 0:
            owner_side = q // (m * cg)
        if g < 3:
            src = xg if g < 2 else dyg

            @pl.when(core == owner_side)
            def _(q=q, g=g, j=j, src=src):
                acc = 0.0
                for h in range(2):
                    acc = acc + dot(u_t[h][g * R : (g + 1) * R], src[h, :, 128 * j : 128 * (j + 1)])
                gsend[(q // cg) % m, q % cg] = acc.astype(bf16)
        else:

            @pl.when(core == owner_side)
            def _(q=q):
                gsend[(q // cg) % m, q % cg] = jnp.zeros((R, 128), bf16)

    loop(1, m, lambda k: g_copy(k, d).start())

    loop(cut2, cut3, lambda c: term_tile(1, c))

    precv[d] = psend[d]
    loop(1, m, lambda k: p_copy(k, other_d(k)).wait_recv())
    total = precv[0].astype(f32)
    for e in range(1, m):
        total = total + precv[e].astype(f32)
    pfin[d] = total.astype(bf16)
    loop(1, m, lambda k: pf_copy(k, d).start())

    loop(cut3, NC, lambda c: term_tile(1, c))
    chip_sum(1, NC - 1)

    grecv[d] = gsend[d]
    loop(1, m, lambda k: g_copy(k, other_d(k)).wait_recv())
    total = grecv[0].astype(f32)
    for e in range(1, m):
        total = total + grecv[e].astype(f32)
    gfin[core, d] = total.astype(bf16)
    loop(1, m, lambda k: gf_copy(k, d).start())
    gd_copy(core, d).start()

    loop(1, m, lambda k: pf_copy(k, other_d(k)).wait_recv())
    for q in range(3 * HC):
        g, j = divmod(q, HC)
        v = pfin[q // cp, q % cp].astype(f32)
        if g < 2:
            p2_ref[g, :, 128 * j : 128 * (j + 1)] = v
        else:
            p1_ref[:, 128 * j : 128 * (j + 1)] = v

    def finish(h, c):
        span = pl.ds(pl.multiple_of(c * W, W), W)
        part = slice(h * S, (h + 1) * S)
        total = term[h, c, core, z].astype(f32) + adapter_scale * dot_nt(u_own[part, : 2 * R], a1_ref[span, :])
        for k in range(1, nz):
            other = lax.rem(z + k, nz)
            rs_copy(h, c, k, other).wait_recv()
            total = total + rsr[h, c, other].astype(f32)
        ig_ref[part, span] = total.astype(bf16)

    loop(0, NC, lambda c: finish(0, c))

    def pass_on(k):
        gf_copy(k, other_d(k)).wait_recv()
        gd_copy(core, other_d(k)).start()

    loop(1, m, pass_on)
    loop(0, m, lambda e: gd_copy(1 - core, e).wait_recv())

    def g_chunk(g, j):
        q = g * DC + j
        return gfin[q // (m * cg), (q // cg) % m, q % cg].astype(f32)

    for j in range(DC):
        both = jnp.concatenate([g_chunk(0, j), g_chunk(1, j)], axis=0)
        first_ref[128 * j : 128 * (j + 1), :] = both.T
        second_ref[:, 128 * j : 128 * (j + 1)] = g_chunk(2, j)

    loop(0, NC, lambda c: finish(1, c))

    for line in lines_x + lines_dy:
        drain(line)
    loop(1, n, lambda k: low_copy(k, t).wait_send())
    loop(1, n, lambda k: ul_copy(k, t).wait_send())
    loop(1, m, lambda k: p_copy(k, d).wait_send())
    loop(1, m, lambda k: pf_copy(k, d).wait_send())
    loop(1, m, lambda k: g_copy(k, d).wait_send())
    loop(1, m, lambda k: gf_copy(k, d).wait_send())
    loop(0, m, lambda e: gd_copy(core, e).wait_send())

    def sent(c):
        for h in range(2):
            die_copy(h, c).wait_send()
            for k in range(1, nz):
                rs_copy(h, c, k, z).wait_send()

    loop(0, NC, sent)


def shards(x, dy, wg, wu, wd, a1, a2, df, d2):
    n = lax.axis_size("tensor")
    m = lax.axis_size("dp")
    T, D = x.shape
    H = wg.shape[1]
    R = a2.shape[1]
    S = T // 2
    GH = n * S
    TW = 256 if H % 256 == 0 else 128
    W = 256
    NC = D // W
    cp = -(-3 * (H // 128) // m)
    cg = -(-3 * (D // 128) // (2 * m))
    factor = adapter_scale / math.sqrt(T * n * m)
    nz = n // 2
    V = pltpu.VMEM
    DMA = pltpu.SemaphoreType.DMA
    any_spec = pl.BlockSpec(memory_space=pl.ANY)
    vmem_spec = pl.BlockSpec(memory_space=pltpu.VMEM)
    macs = 5 * n * T * D * H
    ig, first, second, p2, p1 = pl.pallas_call(
        functools.partial(kernel, n, m, T, H, R, TW, W, cp, cg),
        out_shape=(
            jax.ShapeDtypeStruct((T, D), bf16),
            jax.ShapeDtypeStruct((D, 2 * R), f32),
            jax.ShapeDtypeStruct((R, D), f32),
            jax.ShapeDtypeStruct((2, R, H), f32),
            jax.ShapeDtypeStruct((R, H), f32),
        ),
        in_specs=[any_spec] * 5 + [vmem_spec] * 4,
        out_specs=(vmem_spec,) * 5,
        scratch_shapes=[
            V((2, GH, D), bf16), V((2, GH, D), bf16),
            V((D, H), bf16), V((D, H), bf16), V((H, D), bf16),
            V((GH, H), f32), V((GH, H), f32), V((GH, H), bf16), V((GH, H), bf16),
            V((GH, 2 * R), bf16), V((2 * R, GH), bf16), V((GH, R), bf16), V((R, GH), bf16),
            V((GH, 3 * R), f32), V((n, 2, S, 3 * R), bf16), V((n, 2, S, 3 * R), bf16),
            V((n, 2, S, 3 * R), bf16), V((T, 3 * R), bf16),
            V((3, R, H), f32), V((m, cp, R, 128), bf16), V((m, cp, R, 128), bf16), V((m, cp, R, 128), bf16),
            V((m, cg, R, 128), bf16), V((m, cg, R, 128), bf16), V((2, m, cg, R, 128), bf16),
            V((2, NC, 2, nz, S, W), bf16), V((2, NC, nz, S, W), bf16), V((2, NC, nz, S, W), bf16),
            DMA((7,)),
            DMA((2, 2, n)), DMA((2, n)), DMA((2, 2, n)), DMA((2, n)),
            DMA((n,)), DMA((n,)), DMA((n,)), DMA((n,)),
            DMA((m,)), DMA((m,)), DMA((m,)), DMA((m,)),
            DMA((m,)), DMA((m,)), DMA((m,)), DMA((m,)), DMA((m,)), DMA((m,)),
            DMA((2, NC)), DMA((2, NC)), DMA((2, NC, nz)), DMA((2, NC, nz)),
        ],
        compiler_params=pltpu.CompilerParams(
            collective_id=0, has_side_effects=True, vmem_limit_bytes=63 * 1024 * 1024
        ),
        cost_estimate=pl.CostEstimate(flops=2 * macs, bytes_accessed=6 * D * H, transcendentals=n * T * H),
    )(x, dy, wg, wu, wd, a1, a2, df, d2)
    return ig, factor * first, factor * p2, factor * p1, factor * second


def solution(mesh):
    in_specs = (
        P(("dp", "tensor"), None),
        P(("dp", "tensor"), None),
        P(None, "tensor"),
        P(None, "tensor"),
        P("tensor", None),
        P(),
        P(None, None, "tensor"),
        P(None, "tensor"),
        P(),
    )
    out_specs = (P(("dp", "tensor"), None), P(), P(None, None, "tensor"), P(None, "tensor"), P())
    return jax.shard_map(shards, mesh=mesh, in_specs=in_specs, out_specs=out_specs, check_vma=False)
```

```python
import functools
import math

import jax
import jax.numpy as jnp
from jax import lax
from jax.experimental import pallas as pl
from jax.experimental.pallas import tpu as pltpu
from jax.sharding import PartitionSpec as P

adapter_scale = 0.5
bf16 = jnp.bfloat16
f32 = jnp.float32
MESH = pl.DeviceIdType.MESH


def dot(a, b):
    return jnp.dot(a, b, preferred_element_type=f32)


def dot_nt(a, b):
    return lax.dot_general(a, b, (((1,), (1,)), ((), ())), preferred_element_type=f32)


def kernel(
    n, m, T, H, R, TW, W, cp, cg,
    x_ref, dy_ref, wg_ref, wu_ref, wd_ref, a1_ref, a2_ref, df_ref, d2_ref,
    ig_ref, first_ref, second_ref, p2_ref, p1_ref,
    xg, dyg, wg, wu, wd, gate, up, dgate, dup,
    xlow, xlow_t, dylow, dylow_t, low, lowb, lowr, ulow, u_own,
    pacc, psend, precv, pfin, gsend, grecv, gfin, term, die, rsr,
    load_sem, x_s, x_r, dy_s, dy_r, low_s, low_r, ul_s, ul_r,
    p_s, p_r, pf_s, pf_r, g_s, g_r, gf_s, gf_r, gd_s, gd_r, die_s, die_r, rs_s, rs_r,
):
    t = lax.axis_index("tensor")
    d = lax.axis_index("dp")
    nz = n // 2
    core = lax.rem(t, 2)
    z = lax.div(t, 2)
    partner = t + 1 - 2 * core
    S = T // 2
    D = x_ref.shape[1]
    NC = D // W
    NT = H // TW
    HC = H // 128
    DC = D // 128

    def rows(b):
        return pl.ds(pl.multiple_of(b * S, S), S)

    def loop(lo, hi, body):
        def step(i, carry):
            body(i)
            return carry

        lax.fori_loop(lo, hi, step, 0)

    pairs = []
    for h in range(2):
        part = pl.ds(h * S, S)
        pairs += [(x_ref.at[part], xg.at[h, rows(t)]), (dy_ref.at[part], dyg.at[h, rows(t)])]
    pairs += [(wg_ref, wg), (wu_ref, wu), (wd_ref, wd)]
    loads = [pltpu.make_async_copy(src, dst, load_sem.at[i]) for i, (src, dst) in enumerate(pairs)]
    for c in loads:
        c.start()

    barrier = pltpu.get_barrier_semaphore()
    for k in range(1, n):
        pl.semaphore_signal(barrier, inc=1, device_id={"tensor": lax.rem(t + k, n)}, device_id_type=MESH)
    for k in range(1, m):
        pl.semaphore_signal(barrier, inc=1, device_id={"dp": lax.rem(d + k, m)}, device_id_type=MESH)
    pl.semaphore_wait(barrier, n - 1 + m - 1)

    right = lax.rem(t + 1, n)
    left = lax.rem(t + n - 1, n)

    def hop(line, side, b):
        buf, s_sem, r_sem, h = line
        return pltpu.make_async_remote_copy(
            src_ref=buf.at[h, rows(b)], dst_ref=buf.at[h, rows(b)], send_sem=s_sem.at[h, side, b],
            recv_sem=r_sem.at[h, b], device_id={"tensor": right if side == 0 else left}, device_id_type=MESH,
        )

    def forward(line, s, first=False):
        b = t - s

        @pl.when(b >= 0)
        def _():
            if not first:
                hop(line, 0, b).wait_recv()

            @pl.when(t < n - 1)
            def _():
                hop(line, 0, b).start()

        b2 = t + s

        @pl.when(b2 < n)
        def _():
            if not first:
                hop(line, 1, b2).wait_recv()

            @pl.when(t > 0)
            def _():
                hop(line, 1, b2).start()

    def drain(line):
        def body(b):
            @pl.when(jnp.logical_and(b <= t, t < n - 1))
            def _():
                hop(line, 0, b).wait_send()

            @pl.when(jnp.logical_and(b >= t, t > 0))
            def _():
                hop(line, 1, b).wait_send()

        loop(0, n, body)

    lines_x = [(xg, x_s, x_r, h) for h in range(2)]
    lines_dy = [(dyg, dy_s, dy_r, h) for h in range(2)]

    def tile_cols(j):
        return pl.ds(pl.multiple_of(j * TW, TW), TW)

    def input_rank(h):
        xl = dot(xg[h], a1_ref[...])
        xlow[...] = xl.astype(bf16)
        xlow_t[...] = xl.T.astype(bf16)

    def forward_tile(h, j):
        cols = tile_cols(j)
        gate[:, cols] = dot(xg[h], wg[:, cols]) + adapter_scale * dot(xlow[:, :R], a2_ref[0, :, cols])
        up[:, cols] = dot(xg[h], wu[:, cols]) + adapter_scale * dot(xlow[:, R:], a2_ref[1, :, cols])

    def cotangent_rank(h):
        dl = dot_nt(dyg[h], d2_ref[...])
        dylow[...] = dl.astype(bf16)
        dylow_t[...] = dl.T.astype(bf16)
        low[...] = jnp.zeros_like(low)

    def backward_tile(h, j):
        cols = tile_cols(j)
        dh = dot_nt(dyg[h], wd[cols, :]) + adapter_scale * dot(dylow[...], df_ref[:, cols])
        gp = gate[:, cols]
        u = up[:, cols]
        sig = jax.nn.sigmoid(gp)
        act = gp * sig
        dg = (dh * u * sig * (1.0 + gp * (1.0 - sig))).astype(bf16)
        du = (dh * act).astype(bf16)
        hd = (act * u).astype(bf16)
        dgate[:, cols] = dg
        dup[:, cols] = du
        for i, (a, b) in enumerate([(xlow_t[:R, :], dg), (xlow_t[R:, :], du), (dylow_t[...], hd)]):
            v = dot(a, b)
            if h == 0:
                pacc[i, :, cols] = v
            else:
                pacc[i, :, cols] += v
        low[:, :R] += dot_nt(dg, a2_ref[0, :, cols])
        low[:, R : 2 * R] += dot_nt(du, a2_ref[1, :, cols])
        low[:, 2 * R :] += dot_nt(hd, df_ref[:, cols])

    def keep_low(h):
        lowb[:, h] = low[...].astype(bf16).reshape(n, S, 3 * R)

    def send_to(src, dst, s_sem, r_sem, peer):
        return pltpu.make_async_remote_copy(
            src_ref=src, dst_ref=dst, send_sem=s_sem, recv_sem=r_sem, device_id=peer, device_id_type=MESH
        )

    def low_copy(k, slot):
        peer = lax.rem(t + k, n)
        return send_to(lowb.at[peer], lowr.at[slot], low_s.at[k], low_r.at[slot], {"tensor": peer})

    def ul_copy(k, slot):
        peer = lax.rem(t + k, n)
        return send_to(ulow.at[slot], ulow.at[slot], ul_s.at[k], ul_r.at[slot], {"tensor": peer})

    def scatter_copy(src, dst, s_sem, r_sem, k, slot):
        peer = lax.rem(d + k, m)
        return send_to(src.at[peer], dst.at[slot], s_sem.at[k], r_sem.at[slot], {"dp": peer})

    def p_copy(k, slot):
        return scatter_copy(psend, precv, p_s, p_r, k, slot)

    def g_copy(k, slot):
        return scatter_copy(gsend, grecv, g_s, g_r, k, slot)

    def pf_copy(k, slot):
        peer = lax.rem(d + k, m)
        return send_to(pfin.at[slot], pfin.at[slot], pf_s.at[k], pf_r.at[slot], {"dp": peer})

    def gf_copy(k, slot):
        peer = lax.rem(d + k, m)
        at = gfin.at[core, slot]
        return send_to(at, at, gf_s.at[k], gf_r.at[slot], {"dp": peer})

    def gd_copy(side, slot):
        at = gfin.at[side, slot]
        return send_to(at, at, gd_s.at[slot], gd_r.at[slot], {"tensor": partner})

    def other_d(k):
        return lax.rem(d + k, m)

    def die_copy(h, c):
        return send_to(term.at[h, c, 1 - core], die.at[h, c], die_s.at[h, c], die_r.at[h, c], {"tensor": partner})

    def rs_copy(h, c, b, slot, to):
        return send_to(
            term.at[h, c, core, b], rsr.at[h, c, slot], rs_s.at[h, c, b], rs_r.at[h, c, slot], {"tensor": to}
        )

    lower = lax.rem(t + n - 2, n)
    upper = lax.rem(t + 2, n)

    def chip_sum(h, c):
        die_copy(h, c).wait_recv()
        term[h, c, core] = (term[h, c, core].astype(f32) + die[h, c].astype(f32)).astype(bf16)

    def take(h, c, b, slot, to):
        rs_copy(h, c, b, slot, to).wait_recv()
        term[h, c, core, b] = (term[h, c, core, b].astype(f32) + rsr[h, c, slot].astype(f32)).astype(bf16)

    def downward(h, c):
        @pl.when(z < nz - 1)
        def _():
            loop(0, z + 1, lambda b: take(h, c, b, b, upper))

        loop(0, z, lambda b: rs_copy(h, c, b, b, lower).start())

    def upward(h, c):
        @pl.when(z > 0)
        def _():
            loop(z, nz, lambda b: take(h, c, b, b + 1, lower))

        loop(z + 1, nz, lambda b: rs_copy(h, c, b, b + 1, upper).start())

    NI = NC + nz

    def term_step(h, i):
        @pl.when(i < NC)
        def _():
            span = pl.ds(pl.multiple_of(i * W, W), W)
            v = (dot_nt(dgate[...], wg[span, :]) + dot_nt(dup[...], wu[span, :])).astype(bf16)
            v = v.reshape(nz, 2, S, W)
            term[h, i, 0] = v[:, 0]
            term[h, i, 1] = v[:, 1]
            die_copy(h, i).start()

        c = i - 1

        @pl.when(jnp.logical_and(c >= 0, c < NC))
        def _():
            chip_sum(h, c)

        cd = c - (nz - 1 - z)

        @pl.when(jnp.logical_and(cd >= 0, cd < NC))
        def _():
            downward(h, cd)

        cu = c - z

        @pl.when(jnp.logical_and(cu >= 0, cu < NC))
        def _():
            upward(h, cu)

    loads[0].wait()
    forward(lines_x[0], 0, True)
    loop(1, n, lambda s: forward(lines_x[0], s))
    loads[1].wait()
    forward(lines_dy[0], 0, True)
    input_rank(0)
    loads[4].wait()
    loads[5].wait()

    def beside(line, s, h, tile):
        forward(line, s)

        @pl.when(s - 1 < NT)
        def _():
            tile(h, s - 1)

    loop(1, n, lambda s: beside(lines_dy[0], s, 0, forward_tile))
    loop(n - 1, NT, lambda j: forward_tile(0, j))

    loads[2].wait()
    forward(lines_x[1], 0, True)
    cotangent_rank(0)
    loads[6].wait()
    loop(1, n, lambda s: beside(lines_x[1], s, 0, backward_tile))
    loop(n - 1, NT, lambda j: backward_tile(0, j))

    loads[3].wait()
    forward(lines_dy[1], 0, True)
    keep_low(0)
    input_rank(1)

    def mixed(s):
        forward(lines_dy[1], s)
        term_step(0, s - 1)

        @pl.when(s - 1 < NT)
        def _():
            forward_tile(1, s - 1)

    loop(1, n, mixed)
    loop(n - 1, NT, lambda j: forward_tile(1, j))

    cotangent_rank(1)

    def backward_beside(j):
        backward_tile(1, j)

        @pl.when(n - 1 + j < NI)
        def _():
            term_step(0, n - 1 + j)

    loop(0, NT, backward_beside)
    loop(n - 1 + NT, NI, lambda i: term_step(0, i))
    keep_low(1)

    loop(1, n, lambda k: low_copy(k, t).start())
    for q in range(m * cp):
        g, j = divmod(q, HC)
        if g < 3:
            psend[q // cp, q % cp] = pacc[g, :, 128 * j : 128 * (j + 1)].astype(bf16)
        else:
            psend[q // cp, q % cp] = jnp.zeros((R, 128), bf16)
    loop(1, m, lambda k: p_copy(k, d).start())

    cut1, cut2, cut3 = NI // 5, (2 * NI) // 5, (3 * NI) // 5
    loop(0, cut1, lambda i: term_step(1, i))

    lowr[t] = lowb[t]
    loop(1, n, lambda k: low_copy(k, lax.rem(t + k, n)).wait_recv())
    total = lowr[0].astype(f32)
    for b in range(1, n):
        total = total + lowr[b].astype(f32)
    u_own[...] = total.astype(bf16).reshape(T, 3 * R)
    ulow[t] = total.astype(bf16)
    loop(1, n, lambda k: ul_copy(k, t).start())

    loop(cut1, cut2, lambda i: term_step(1, i))

    loop(1, n, lambda k: ul_copy(k, lax.rem(t + k, n)).wait_recv())
    u_t = [ulow[:, h].reshape(n * S, 3 * R).astype(f32).T.astype(bf16) for h in range(2)]
    for q in range(2 * m * cg):
        g, j = divmod(q, DC)
        if q % (m * cg) == 0:
            owner_side = q // (m * cg)
        if g < 3:
            src = xg if g < 2 else dyg

            @pl.when(core == owner_side)
            def _(q=q, g=g, j=j, src=src):
                acc = 0.0
                for h in range(2):
                    acc = acc + dot(u_t[h][g * R : (g + 1) * R], src[h, :, 128 * j : 128 * (j + 1)])
                gsend[(q // cg) % m, q % cg] = acc.astype(bf16)
        else:

            @pl.when(core == owner_side)
            def _(q=q):
                gsend[(q // cg) % m, q % cg] = jnp.zeros((R, 128), bf16)

    loop(1, m, lambda k: g_copy(k, d).start())

    loop(cut2, cut3, lambda i: term_step(1, i))

    precv[d] = psend[d]
    loop(1, m, lambda k: p_copy(k, other_d(k)).wait_recv())
    total = precv[0].astype(f32)
    for e in range(1, m):
        total = total + precv[e].astype(f32)
    pfin[d] = total.astype(bf16)
    loop(1, m, lambda k: pf_copy(k, d).start())

    loop(cut3, NI, lambda i: term_step(1, i))

    grecv[d] = gsend[d]
    loop(1, m, lambda k: g_copy(k, other_d(k)).wait_recv())
    total = grecv[0].astype(f32)
    for e in range(1, m):
        total = total + grecv[e].astype(f32)
    gfin[core, d] = total.astype(bf16)
    loop(1, m, lambda k: gf_copy(k, d).start())
    gd_copy(core, d).start()

    loop(1, m, lambda k: pf_copy(k, other_d(k)).wait_recv())
    for q in range(3 * HC):
        g, j = divmod(q, HC)
        v = pfin[q // cp, q % cp].astype(f32)
        if g < 2:
            p2_ref[g, :, 128 * j : 128 * (j + 1)] = v
        else:
            p1_ref[:, 128 * j : 128 * (j + 1)] = v

    def finish(h, c):
        span = pl.ds(pl.multiple_of(c * W, W), W)
        part = slice(h * S, (h + 1) * S)
        total = term[h, c, core, z].astype(f32) + adapter_scale * dot_nt(u_own[part, : 2 * R], a1_ref[span, :])
        ig_ref[part, span] = total.astype(bf16)

    loop(0, NC, lambda c: finish(0, c))

    def pass_on(k):
        gf_copy(k, other_d(k)).wait_recv()
        gd_copy(core, other_d(k)).start()

    loop(1, m, pass_on)
    loop(0, m, lambda e: gd_copy(1 - core, e).wait_recv())

    def g_chunk(g, j):
        q = g * DC + j
        return gfin[q // (m * cg), (q // cg) % m, q % cg].astype(f32)

    for j in range(DC):
        both = jnp.concatenate([g_chunk(0, j), g_chunk(1, j)], axis=0)
        first_ref[128 * j : 128 * (j + 1), :] = both.T
        second_ref[:, 128 * j : 128 * (j + 1)] = g_chunk(2, j)

    loop(0, NC, lambda c: finish(1, c))

    for line in lines_x + lines_dy:
        drain(line)
    loop(1, n, lambda k: low_copy(k, t).wait_send())
    loop(1, n, lambda k: ul_copy(k, t).wait_send())
    loop(1, m, lambda k: p_copy(k, d).wait_send())
    loop(1, m, lambda k: pf_copy(k, d).wait_send())
    loop(1, m, lambda k: g_copy(k, d).wait_send())
    loop(1, m, lambda k: gf_copy(k, d).wait_send())
    loop(0, m, lambda e: gd_copy(core, e).wait_send())

    def sent(c):
        for h in range(2):
            die_copy(h, c).wait_send()
            loop(0, z, lambda b: rs_copy(h, c, b, b, lower).wait_send())
            loop(z + 1, nz, lambda b: rs_copy(h, c, b, b + 1, upper).wait_send())

    loop(0, NC, sent)


def shards(x, dy, wg, wu, wd, a1, a2, df, d2):
    n = lax.axis_size("tensor")
    m = lax.axis_size("dp")
    T, D = x.shape
    H = wg.shape[1]
    R = a2.shape[1]
    S = T // 2
    GH = n * S
    TW = 256 if H % 256 == 0 else 128
    W = 512 if D % 512 == 0 else 256
    NC = D // W
    cp = -(-3 * (H // 128) // m)
    cg = -(-3 * (D // 128) // (2 * m))
    factor = adapter_scale / math.sqrt(T * n * m)
    nz = n // 2
    V = pltpu.VMEM
    DMA = pltpu.SemaphoreType.DMA
    any_spec = pl.BlockSpec(memory_space=pl.ANY)
    vmem_spec = pl.BlockSpec(memory_space=pltpu.VMEM)
    macs = 5 * n * T * D * H
    ig, first, second, p2, p1 = pl.pallas_call(
        functools.partial(kernel, n, m, T, H, R, TW, W, cp, cg),
        out_shape=(
            jax.ShapeDtypeStruct((T, D), bf16),
            jax.ShapeDtypeStruct((D, 2 * R), f32),
            jax.ShapeDtypeStruct((R, D), f32),
            jax.ShapeDtypeStruct((2, R, H), f32),
            jax.ShapeDtypeStruct((R, H), f32),
        ),
        in_specs=[any_spec] * 5 + [vmem_spec] * 4,
        out_specs=(vmem_spec,) * 5,
        scratch_shapes=[
            V((2, GH, D), bf16), V((2, GH, D), bf16),
            V((D, H), bf16), V((D, H), bf16), V((H, D), bf16),
            V((GH, H), f32), V((GH, H), f32), V((GH, H), bf16), V((GH, H), bf16),
            V((GH, 2 * R), bf16), V((2 * R, GH), bf16), V((GH, R), bf16), V((R, GH), bf16),
            V((GH, 3 * R), f32), V((n, 2, S, 3 * R), bf16), V((n, 2, S, 3 * R), bf16),
            V((n, 2, S, 3 * R), bf16), V((T, 3 * R), bf16),
            V((3, R, H), f32), V((m, cp, R, 128), bf16), V((m, cp, R, 128), bf16), V((m, cp, R, 128), bf16),
            V((m, cg, R, 128), bf16), V((m, cg, R, 128), bf16), V((2, m, cg, R, 128), bf16),
            V((2, NC, 2, nz, S, W), bf16), V((2, NC, nz, S, W), bf16), V((2, NC, nz + 1, S, W), bf16),
            DMA((7,)),
            DMA((2, 2, n)), DMA((2, n)), DMA((2, 2, n)), DMA((2, n)),
            DMA((n,)), DMA((n,)), DMA((n,)), DMA((n,)),
            DMA((m,)), DMA((m,)), DMA((m,)), DMA((m,)),
            DMA((m,)), DMA((m,)), DMA((m,)), DMA((m,)), DMA((m,)), DMA((m,)),
            DMA((2, NC)), DMA((2, NC)), DMA((2, NC, nz)), DMA((2, NC, nz + 1)),
        ],
        compiler_params=pltpu.CompilerParams(
            collective_id=0, has_side_effects=True, vmem_limit_bytes=63 * 1024 * 1024
        ),
        cost_estimate=pl.CostEstimate(flops=2 * macs, bytes_accessed=6 * D * H, transcendentals=n * T * H),
    )(x, dy, wg, wu, wd, a1, a2, df, d2)
    return ig, factor * first, factor * p2, factor * p1, factor * second


def solution(mesh):
    in_specs = (
        P(("dp", "tensor"), None),
        P(("dp", "tensor"), None),
        P(None, "tensor"),
        P(None, "tensor"),
        P("tensor", None),
        P(),
        P(None, None, "tensor"),
        P(None, "tensor"),
        P(),
    )
    out_specs = (P(("dp", "tensor"), None), P(), P(None, None, "tensor"), P(None, "tensor"), P())
    return jax.shard_map(shards, mesh=mesh, in_specs=in_specs, out_specs=out_specs, check_vma=False)
```

```python
import functools
import math

import jax
import jax.numpy as jnp
from jax import lax
from jax.experimental import pallas as pl
from jax.experimental.pallas import tpu as pltpu
from jax.sharding import PartitionSpec as P

adapter_scale = 0.5
bf16 = jnp.bfloat16
f32 = jnp.float32
MESH = pl.DeviceIdType.MESH


def dot(a, b):
    return jnp.dot(a, b, preferred_element_type=f32)


def dot_nt(a, b):
    return lax.dot_general(a, b, (((1,), (1,)), ((), ())), preferred_element_type=f32)


def kernel(
    n, m, T, H, R, TW, W, cp, cg,
    x_ref, dy_ref, wg_ref, wu_ref, wd_ref, a1_ref, a2_ref, df_ref, d2_ref,
    ig_ref, first_ref, second_ref, p2_ref, p1_ref,
    xg, dyg, wg, wu, wd, gate, up, dgate, dup,
    xlow, xlow_t, dylow, dylow_t, low, lowb, lowr, ulow, u_own,
    dhid, hid, ulow_t, pacc, psend, precv, pfin, gsend, grecv, gfin, term, die, rsr,
    load_sem, x_s, x_r, dy_s, dy_r, low_s, low_r, ul_s, ul_r,
    p_s, p_r, pf_s, pf_r, g_s, g_r, gf_s, gf_r, gd_s, gd_r, die_s, die_r, rs_s, rs_r,
):
    t = lax.axis_index("tensor")
    d = lax.axis_index("dp")
    nz = n // 2
    core = lax.rem(t, 2)
    z = lax.div(t, 2)
    partner = t + 1 - 2 * core
    S = T // 2
    D = x_ref.shape[1]
    NC = D // W
    NT = H // TW
    KC = W
    NK = D // KC
    HC = H // 128
    DC = D // 128

    def rows(b):
        return pl.ds(pl.multiple_of(b * S, S), S)

    def loop(lo, hi, body):
        def step(i, carry):
            body(i)
            return carry

        lax.fori_loop(lo, hi, step, 0)

    pairs = []
    for h in range(2):
        part = pl.ds(h * S, S)
        pairs += [(x_ref.at[part], xg.at[h, rows(t)]), (dy_ref.at[part], dyg.at[h, rows(t)])]
    pairs += [(wg_ref, wg), (wu_ref, wu), (wd_ref, wd)]
    loads = [pltpu.make_async_copy(src, dst, load_sem.at[i]) for i, (src, dst) in enumerate(pairs)]
    for c in loads:
        c.start()

    barrier = pltpu.get_barrier_semaphore()
    for k in range(1, n):
        pl.semaphore_signal(barrier, inc=1, device_id={"tensor": lax.rem(t + k, n)}, device_id_type=MESH)
    for k in range(1, m):
        pl.semaphore_signal(barrier, inc=1, device_id={"dp": lax.rem(d + k, m)}, device_id_type=MESH)
    pl.semaphore_wait(barrier, n - 1 + m - 1)

    right = lax.rem(t + 1, n)
    left = lax.rem(t + n - 1, n)

    def hop(line, side, b):
        buf, s_sem, r_sem, h = line
        return pltpu.make_async_remote_copy(
            src_ref=buf.at[h, rows(b)], dst_ref=buf.at[h, rows(b)], send_sem=s_sem.at[h, side, b],
            recv_sem=r_sem.at[h, b], device_id={"tensor": right if side == 0 else left}, device_id_type=MESH,
        )

    def forward(line, s, first=False):
        b = t - s

        @pl.when(b >= 0)
        def _():
            if not first:
                hop(line, 0, b).wait_recv()

            @pl.when(t < n - 1)
            def _():
                hop(line, 0, b).start()

        b2 = t + s

        @pl.when(b2 < n)
        def _():
            if not first:
                hop(line, 1, b2).wait_recv()

            @pl.when(t > 0)
            def _():
                hop(line, 1, b2).start()

    def drain(line):
        def body(b):
            @pl.when(jnp.logical_and(b <= t, t < n - 1))
            def _():
                hop(line, 0, b).wait_send()

            @pl.when(jnp.logical_and(b >= t, t > 0))
            def _():
                hop(line, 1, b).wait_send()

        loop(0, n, body)

    lines_x = [(xg, x_s, x_r, h) for h in range(2)]
    lines_dy = [(dyg, dy_s, dy_r, h) for h in range(2)]

    def tile_cols(j):
        return pl.ds(pl.multiple_of(j * TW, TW), TW)

    def input_rank(h):
        xl = dot(xg[h], a1_ref[...])
        xlow[...] = xl.astype(bf16)
        xlow_t[...] = xl.T.astype(bf16)

    def depth(k):
        return pl.ds(pl.multiple_of(k * KC, KC), KC)

    def forward_start():
        gate[...] = adapter_scale * dot(xlow[:, :R], a2_ref[0])
        up[...] = adapter_scale * dot(xlow[:, R:], a2_ref[1])

    def forward_part(h, k):
        a = xg[h, :, depth(k)]
        gate[...] += dot(a, wg[depth(k), :])
        up[...] += dot(a, wu[depth(k), :])

    def cotangent_rank(h):
        dl = dot_nt(dyg[h], d2_ref[...])
        dylow[...] = dl.astype(bf16)
        dylow_t[...] = dl.T.astype(bf16)
        dhid[...] = adapter_scale * dot(dylow[...], df_ref[...])

    def backward_part(h, k):
        dhid[...] += dot_nt(dyg[h, :, depth(k)], wd[:, depth(k)])

    def pointwise(j):
        cols = tile_cols(j)
        dh = dhid[:, cols]
        gp = gate[:, cols]
        u = up[:, cols]
        sig = jax.nn.sigmoid(gp)
        act = gp * sig
        dgate[:, cols] = (dh * u * sig * (1.0 + gp * (1.0 - sig))).astype(bf16)
        dup[:, cols] = (dh * act).astype(bf16)
        hid[:, cols] = (act * u).astype(bf16)

    def rank_products(h):
        for i, (a, b) in enumerate([(xlow_t[:R, :], dgate), (xlow_t[R:, :], dup), (dylow_t[...], hid)]):
            v = dot(a, b[...])
            if h == 0:
                pacc[i] = v
            else:
                pacc[i] += v
        low[:, :R] = dot_nt(dgate[...], a2_ref[0])
        low[:, R : 2 * R] = dot_nt(dup[...], a2_ref[1])
        low[:, 2 * R :] = dot_nt(hid[...], df_ref[...])
        keep_low(h)

    def keep_low(h):
        lowb[:, h] = low[...].astype(bf16).reshape(n, S, 3 * R)

    def send_to(src, dst, s_sem, r_sem, peer):
        return pltpu.make_async_remote_copy(
            src_ref=src, dst_ref=dst, send_sem=s_sem, recv_sem=r_sem, device_id=peer, device_id_type=MESH
        )

    def low_copy(k, slot):
        peer = lax.rem(t + k, n)
        return send_to(lowb.at[peer], lowr.at[slot], low_s.at[k], low_r.at[slot], {"tensor": peer})

    def ul_copy(k, slot):
        peer = lax.rem(t + k, n)
        return send_to(ulow.at[slot], ulow.at[slot], ul_s.at[k], ul_r.at[slot], {"tensor": peer})

    def scatter_copy(src, dst, s_sem, r_sem, k, slot):
        peer = lax.rem(d + k, m)
        return send_to(src.at[peer], dst.at[slot], s_sem.at[k], r_sem.at[slot], {"dp": peer})

    def p_copy(k, slot):
        return scatter_copy(psend, precv, p_s, p_r, k, slot)

    def g_part(e):
        return pl.ds((core * m + e) * cg, cg)

    def g_copy(k, slot):
        peer = lax.rem(d + k, m)
        return send_to(gsend.at[g_part(peer)], grecv.at[slot], g_s.at[k], g_r.at[slot], {"dp": peer})

    def pf_copy(k, slot):
        peer = lax.rem(d + k, m)
        return send_to(pfin.at[slot], pfin.at[slot], pf_s.at[k], pf_r.at[slot], {"dp": peer})

    def gf_copy(k, slot):
        peer = lax.rem(d + k, m)
        at = gfin.at[core, slot]
        return send_to(at, at, gf_s.at[k], gf_r.at[slot], {"dp": peer})

    def gd_copy(side, slot):
        at = gfin.at[side, slot]
        return send_to(at, at, gd_s.at[slot], gd_r.at[slot], {"tensor": partner})

    def other_d(k):
        return lax.rem(d + k, m)

    def die_copy(h, c):
        return send_to(term.at[h, c, 1 - core], die.at[h, c], die_s.at[h, c], die_r.at[h, c], {"tensor": partner})

    def rs_copy(h, c, b, slot, to):
        return send_to(
            term.at[h, c, core, b], rsr.at[h, c, slot], rs_s.at[h, c, b], rs_r.at[h, c, slot], {"tensor": to}
        )

    lower = lax.rem(t + n - 2, n)
    upper = lax.rem(t + 2, n)

    def chip_sum(h, c):
        die_copy(h, c).wait_recv()
        term[h, c, core] = (term[h, c, core].astype(f32) + die[h, c].astype(f32)).astype(bf16)

    def take(h, c, b, slot, to):
        rs_copy(h, c, b, slot, to).wait_recv()
        term[h, c, core, b] = (term[h, c, core, b].astype(f32) + rsr[h, c, slot].astype(f32)).astype(bf16)

    def downward(h, c):
        @pl.when(z < nz - 1)
        def _():
            loop(0, z + 1, lambda b: take(h, c, b, b, upper))

        loop(0, z, lambda b: rs_copy(h, c, b, b, lower).start())

    def upward(h, c):
        @pl.when(z > 0)
        def _():
            loop(z, nz, lambda b: take(h, c, b, b + 1, lower))

        loop(z + 1, nz, lambda b: rs_copy(h, c, b, b + 1, upper).start())

    NI = NC + nz

    def term_step(h, i):
        @pl.when(i < NC)
        def _():
            span = pl.ds(pl.multiple_of(i * W, W), W)
            v = (dot_nt(dgate[...], wg[span, :]) + dot_nt(dup[...], wu[span, :])).astype(bf16)
            v = v.reshape(nz, 2, S, W)
            term[h, i, 0] = v[:, 0]
            term[h, i, 1] = v[:, 1]
            die_copy(h, i).start()

        c = i - 1

        @pl.when(jnp.logical_and(c >= 0, c < NC))
        def _():
            chip_sum(h, c)

        cd = c - (nz - 1 - z)

        @pl.when(jnp.logical_and(cd >= 0, cd < NC))
        def _():
            downward(h, cd)

        cu = c - z

        @pl.when(jnp.logical_and(cu >= 0, cu < NC))
        def _():
            upward(h, cu)

    loads[0].wait()
    forward(lines_x[0], 0, True)
    loop(1, n, lambda s: forward(lines_x[0], s))
    loads[1].wait()
    forward(lines_dy[0], 0, True)
    input_rank(0)
    forward_start()
    loads[4].wait()
    loads[5].wait()

    def beside(line, s, h, tile):
        forward(line, s)

        @pl.when(s - 1 < NK)
        def _():
            tile(h, s - 1)

    loop(1, n, lambda s: beside(lines_dy[0], s, 0, forward_part))
    loop(n - 1, NK, lambda j: forward_part(0, j))

    loads[2].wait()
    forward(lines_x[1], 0, True)
    cotangent_rank(0)
    loads[6].wait()
    loop(1, n, lambda s: beside(lines_x[1], s, 0, backward_part))
    loop(n - 1, NK, lambda j: backward_part(0, j))
    loop(0, NT, pointwise)
    rank_products(0)

    loads[3].wait()
    forward(lines_dy[1], 0, True)
    input_rank(1)
    forward_start()

    def mixed(s):
        forward(lines_dy[1], s)
        term_step(0, s - 1)

        @pl.when(s - 1 < NK)
        def _():
            forward_part(1, s - 1)

    loop(1, n, mixed)
    loop(n - 1, NK, lambda j: forward_part(1, j))

    cotangent_rank(1)

    def backward_beside(j):
        backward_part(1, j)

        @pl.when(n - 1 + j < NI)
        def _():
            term_step(0, n - 1 + j)

    loop(0, NK, backward_beside)
    loop(n - 1 + NK, NI, lambda i: term_step(0, i))
    loop(0, NT, pointwise)
    rank_products(1)

    loop(1, n, lambda k: low_copy(k, t).start())
    for q in range(m * cp):
        g, j = divmod(q, HC)
        if g < 3:
            psend[q // cp, q % cp] = pacc[g, :, 128 * j : 128 * (j + 1)].astype(bf16)
        else:
            psend[q // cp, q % cp] = jnp.zeros((R, 128), bf16)
    loop(1, m, lambda k: p_copy(k, d).start())

    cut1, cut2, cut3 = NI // 5, (2 * NI) // 5, (3 * NI) // 5
    loop(0, cut1, lambda i: term_step(1, i))

    lowr[t] = lowb[t]
    loop(1, n, lambda k: low_copy(k, lax.rem(t + k, n)).wait_recv())
    total = lowr[0].astype(f32)
    for b in range(1, n):
        total = total + lowr[b].astype(f32)
    u_own[...] = total.astype(bf16).reshape(T, 3 * R)
    ulow[t] = total.astype(bf16)
    loop(1, n, lambda k: ul_copy(k, t).start())

    loop(cut1, cut2, lambda i: term_step(1, i))

    loop(1, n, lambda k: ul_copy(k, lax.rem(t + k, n)).wait_recv())
    for h in range(2):
        ulow_t[h] = ulow[:, h].reshape(n * S, 3 * R).astype(f32).T.astype(bf16)
    u_t = [ulow_t.at[h] for h in range(2)]
    for q in range(3 * DC, 2 * m * cg):
        gsend[q] = jnp.zeros((R, 128), bf16)

    def factor_part(k):
        for src, lo, hi in ((xg, 0, 2), (dyg, 2, 3)):
            v = dot(u_t[0][lo * R : hi * R], src[0, :, depth(k)]) + dot(u_t[1][lo * R : hi * R], src[1, :, depth(k)])
            for g in range(lo, hi):
                for i in range(KC // 128):
                    gsend[g * DC + k * (KC // 128) + i] = v[
                        (g - lo) * R : (g - lo + 1) * R, 128 * i : 128 * (i + 1)
                    ].astype(bf16)

    loop(0, NK, factor_part)
    loop(1, m, lambda k: g_copy(k, d).start())

    loop(cut2, cut3, lambda i: term_step(1, i))

    precv[d] = psend[d]
    loop(1, m, lambda k: p_copy(k, other_d(k)).wait_recv())
    total = precv[0].astype(f32)
    for e in range(1, m):
        total = total + precv[e].astype(f32)
    pfin[d] = total.astype(bf16)
    loop(1, m, lambda k: pf_copy(k, d).start())

    loop(cut3, NI, lambda i: term_step(1, i))

    grecv[d] = gsend[g_part(d)]
    loop(1, m, lambda k: g_copy(k, other_d(k)).wait_recv())
    total = grecv[0].astype(f32)
    for e in range(1, m):
        total = total + grecv[e].astype(f32)
    gfin[core, d] = total.astype(bf16)
    loop(1, m, lambda k: gf_copy(k, d).start())
    gd_copy(core, d).start()

    loop(1, m, lambda k: pf_copy(k, other_d(k)).wait_recv())
    for q in range(3 * HC):
        g, j = divmod(q, HC)
        v = pfin[q // cp, q % cp].astype(f32)
        if g < 2:
            p2_ref[g, :, 128 * j : 128 * (j + 1)] = v
        else:
            p1_ref[:, 128 * j : 128 * (j + 1)] = v

    def finish(h, c):
        span = pl.ds(pl.multiple_of(c * W, W), W)
        part = slice(h * S, (h + 1) * S)
        total = term[h, c, core, z].astype(f32) + adapter_scale * dot_nt(u_own[part, : 2 * R], a1_ref[span, :])
        ig_ref[part, span] = total.astype(bf16)

    loop(0, NC, lambda c: finish(0, c))

    def pass_on(k):
        gf_copy(k, other_d(k)).wait_recv()
        gd_copy(core, other_d(k)).start()

    loop(1, m, pass_on)
    loop(0, m, lambda e: gd_copy(1 - core, e).wait_recv())

    def g_chunk(g, j):
        q = g * DC + j
        return gfin[q // (m * cg), (q // cg) % m, q % cg].astype(f32)

    for j in range(DC):
        both = jnp.concatenate([g_chunk(0, j), g_chunk(1, j)], axis=0)
        first_ref[128 * j : 128 * (j + 1), :] = both.T
        second_ref[:, 128 * j : 128 * (j + 1)] = g_chunk(2, j)

    loop(0, NC, lambda c: finish(1, c))

    for line in lines_x + lines_dy:
        drain(line)
    loop(1, n, lambda k: low_copy(k, t).wait_send())
    loop(1, n, lambda k: ul_copy(k, t).wait_send())
    loop(1, m, lambda k: p_copy(k, d).wait_send())
    loop(1, m, lambda k: pf_copy(k, d).wait_send())
    loop(1, m, lambda k: g_copy(k, d).wait_send())
    loop(1, m, lambda k: gf_copy(k, d).wait_send())
    loop(0, m, lambda e: gd_copy(core, e).wait_send())

    def sent(c):
        for h in range(2):
            die_copy(h, c).wait_send()
            loop(0, z, lambda b: rs_copy(h, c, b, b, lower).wait_send())
            loop(z + 1, nz, lambda b: rs_copy(h, c, b, b + 1, upper).wait_send())

    loop(0, NC, sent)


def shards(x, dy, wg, wu, wd, a1, a2, df, d2):
    n = lax.axis_size("tensor")
    m = lax.axis_size("dp")
    T, D = x.shape
    H = wg.shape[1]
    R = a2.shape[1]
    S = T // 2
    GH = n * S
    TW = 256 if H % 256 == 0 else 128
    W = 512 if D % 512 == 0 else 256
    NC = D // W
    cp = -(-3 * (H // 128) // m)
    cg = -(-3 * (D // 128) // (2 * m))
    factor = adapter_scale / math.sqrt(T * n * m)
    nz = n // 2
    V = pltpu.VMEM
    DMA = pltpu.SemaphoreType.DMA
    any_spec = pl.BlockSpec(memory_space=pl.ANY)
    vmem_spec = pl.BlockSpec(memory_space=pltpu.VMEM)
    macs = 5 * n * T * D * H
    ig, first, second, p2, p1 = pl.pallas_call(
        functools.partial(kernel, n, m, T, H, R, TW, W, cp, cg),
        out_shape=(
            jax.ShapeDtypeStruct((T, D), bf16),
            jax.ShapeDtypeStruct((D, 2 * R), f32),
            jax.ShapeDtypeStruct((R, D), f32),
            jax.ShapeDtypeStruct((2, R, H), f32),
            jax.ShapeDtypeStruct((R, H), f32),
        ),
        in_specs=[any_spec] * 5 + [vmem_spec] * 4,
        out_specs=(vmem_spec,) * 5,
        scratch_shapes=[
            V((2, GH, D), bf16), V((2, GH, D), bf16),
            V((D, H), bf16), V((D, H), bf16), V((H, D), bf16),
            V((GH, H), f32), V((GH, H), f32), V((GH, H), bf16), V((GH, H), bf16),
            V((GH, 2 * R), bf16), V((2 * R, GH), bf16), V((GH, R), bf16), V((R, GH), bf16),
            V((GH, 3 * R), f32), V((n, 2, S, 3 * R), bf16), V((n, 2, S, 3 * R), bf16),
            V((n, 2, S, 3 * R), bf16), V((T, 3 * R), bf16),
            V((GH, H), f32), V((GH, H), bf16), V((2, 3 * R, GH), bf16),
            V((3, R, H), f32), V((m, cp, R, 128), bf16), V((m, cp, R, 128), bf16), V((m, cp, R, 128), bf16),
            V((2 * m * cg, R, 128), bf16), V((m, cg, R, 128), bf16), V((2, m, cg, R, 128), bf16),
            V((2, NC, 2, nz, S, W), bf16), V((2, NC, nz, S, W), bf16), V((2, NC, nz + 1, S, W), bf16),
            DMA((7,)),
            DMA((2, 2, n)), DMA((2, n)), DMA((2, 2, n)), DMA((2, n)),
            DMA((n,)), DMA((n,)), DMA((n,)), DMA((n,)),
            DMA((m,)), DMA((m,)), DMA((m,)), DMA((m,)),
            DMA((m,)), DMA((m,)), DMA((m,)), DMA((m,)), DMA((m,)), DMA((m,)),
            DMA((2, NC)), DMA((2, NC)), DMA((2, NC, nz)), DMA((2, NC, nz + 1)),
        ],
        compiler_params=pltpu.CompilerParams(
            collective_id=0, has_side_effects=True, vmem_limit_bytes=63 * 1024 * 1024
        ),
        cost_estimate=pl.CostEstimate(flops=2 * macs, bytes_accessed=6 * D * H, transcendentals=n * T * H),
    )(x, dy, wg, wu, wd, a1, a2, df, d2)
    return ig, factor * first, factor * p2, factor * p1, factor * second


def solution(mesh):
    in_specs = (
        P(("dp", "tensor"), None),
        P(("dp", "tensor"), None),
        P(None, "tensor"),
        P(None, "tensor"),
        P("tensor", None),
        P(),
        P(None, None, "tensor"),
        P(None, "tensor"),
        P(),
    )
    out_specs = (P(("dp", "tensor"), None), P(), P(None, None, "tensor"), P(None, "tensor"), P())
    return jax.shard_map(shards, mesh=mesh, in_specs=in_specs, out_specs=out_specs, check_vma=False)
```

```python
import functools
import math

import jax
import jax.numpy as jnp
from jax import lax
from jax.experimental import pallas as pl
from jax.experimental.pallas import tpu as pltpu
from jax.sharding import PartitionSpec as P

adapter_scale = 0.5
bf16 = jnp.bfloat16
f32 = jnp.float32
MESH = pl.DeviceIdType.MESH


def dot(a, b):
    return jnp.dot(a, b, preferred_element_type=f32)


def dot_nt(a, b):
    return lax.dot_general(a, b, (((1,), (1,)), ((), ())), preferred_element_type=f32)


def kernel(
    n, m, T, H, R, TW, W, cp, cg,
    x_ref, dy_ref, wg_ref, wu_ref, wd_ref, a1_ref, a2_ref, df_ref, d2_ref,
    ig_ref, first_ref, second_ref, p2_ref, p1_ref,
    xg, dyg, wg, wu, wd, gate, up, dgate, dup,
    xlow, xlow_t, dylow, dylow_t, low, lowb, lowr, ulow, u_own,
    pacc, psend, precv, pfin, gsend, grecv, gfin, term, die, rsr,
    load_sem, x_s, x_r, dy_s, dy_r, low_s, low_r, ul_s, ul_r,
    p_s, p_r, pf_s, pf_r, g_s, g_r, gf_s, gf_r, gd_s, gd_r, die_s, die_r, rs_s, rs_r,
):
    t = lax.axis_index("tensor")
    d = lax.axis_index("dp")
    nz = n // 2
    core = lax.rem(t, 2)
    z = lax.div(t, 2)
    partner = t + 1 - 2 * core
    S = T // 2
    D = x_ref.shape[1]
    NC = D // W
    NT = H // TW
    HC = H // 128
    DC = D // 128

    def rows(b):
        return pl.ds(pl.multiple_of(b * S, S), S)

    def loop(lo, hi, body):
        def step(i, carry):
            body(i)
            return carry

        lax.fori_loop(lo, hi, step, 0)

    pairs = []
    for h in range(2):
        part = pl.ds(h * S, S)
        pairs += [(x_ref.at[part], xg.at[h, rows(t)]), (dy_ref.at[part], dyg.at[h, rows(t)])]
    pairs += [(wg_ref, wg), (wu_ref, wu), (wd_ref, wd)]
    loads = [pltpu.make_async_copy(src, dst, load_sem.at[i]) for i, (src, dst) in enumerate(pairs)]
    for c in loads:
        c.start()

    barrier = pltpu.get_barrier_semaphore()
    for k in range(1, n):
        pl.semaphore_signal(barrier, inc=1, device_id={"tensor": lax.rem(t + k, n)}, device_id_type=MESH)
    for k in range(1, m):
        pl.semaphore_signal(barrier, inc=1, device_id={"dp": lax.rem(d + k, m)}, device_id_type=MESH)
    pl.semaphore_wait(barrier, n - 1 + m - 1)

    toward = (lax.rem(t + 2, n), lax.rem(t + n - 2, n), partner)

    def hop(line, side, b):
        buf, s_sem, r_sem, h = line
        return pltpu.make_async_remote_copy(
            src_ref=buf.at[h, rows(b)], dst_ref=buf.at[h, rows(b)], send_sem=s_sem.at[h, side, b],
            recv_sem=r_sem.at[h, b], device_id={"tensor": toward[side]}, device_id_type=MESH,
        )

    def start(line):
        @pl.when(z < nz - 1)
        def _():
            hop(line, 0, t).start()

        @pl.when(z > 0)
        def _():
            hop(line, 1, t).start()

        hop(line, 2, t).start()

    def relay(line, s):
        @pl.when(z >= s)
        def _():
            b = t - 2 * s
            hop(line, 0, b).wait_recv()

            @pl.when(z < nz - 1)
            def _():
                hop(line, 0, b).start()

            hop(line, 2, b).start()

        @pl.when(z + s < nz)
        def _():
            b = t + 2 * s
            hop(line, 1, b).wait_recv()

            @pl.when(z > 0)
            def _():
                hop(line, 1, b).start()

            hop(line, 2, b).start()

    def collect(line, s):
        @pl.when(z >= s)
        def _():
            hop(line, 2, partner - 2 * s).wait_recv()

        @pl.when(jnp.logical_and(z + s < nz, s > 0))
        def _():
            hop(line, 2, partner + 2 * s).wait_recv()

    def forward(line, i):
        odd = lax.rem(i, 2) == 1

        @pl.when(jnp.logical_and(odd, i < n - 1))
        def _():
            relay(line, lax.div(i + 1, 2))

        @pl.when(lax.rem(i, 2) == 0)
        def _():
            collect(line, lax.div(i, 2))

        @pl.when(i == n - 1)
        def _():
            collect(line, 0)

    def drain(line):
        def body(zb):
            b = 2 * zb + core

            @pl.when(jnp.logical_and(zb <= z, z < nz - 1))
            def _():
                hop(line, 0, b).wait_send()

            @pl.when(jnp.logical_and(zb >= z, z > 0))
            def _():
                hop(line, 1, b).wait_send()

            hop(line, 2, b).wait_send()

        loop(0, nz, body)

    lines_x = [(xg, x_s, x_r, h) for h in range(2)]
    lines_dy = [(dyg, dy_s, dy_r, h) for h in range(2)]

    def tile_cols(j):
        return pl.ds(pl.multiple_of(j * TW, TW), TW)

    def input_rank(h):
        xl = dot(xg[h], a1_ref[...])
        xlow[...] = xl.astype(bf16)
        xlow_t[...] = xl.T.astype(bf16)

    def forward_tile(h, j):
        cols = tile_cols(j)
        gate[:, cols] = dot(xg[h], wg[:, cols]) + adapter_scale * dot(xlow[:, :R], a2_ref[0, :, cols])
        up[:, cols] = dot(xg[h], wu[:, cols]) + adapter_scale * dot(xlow[:, R:], a2_ref[1, :, cols])

    def cotangent_rank(h):
        dl = dot_nt(dyg[h], d2_ref[...])
        dylow[...] = dl.astype(bf16)
        dylow_t[...] = dl.T.astype(bf16)
        low[...] = jnp.zeros_like(low)

    def backward_tile(h, j):
        cols = tile_cols(j)
        dh = dot_nt(dyg[h], wd[cols, :]) + adapter_scale * dot(dylow[...], df_ref[:, cols])
        gp = gate[:, cols]
        u = up[:, cols]
        sig = jax.nn.sigmoid(gp)
        act = gp * sig
        dg = (dh * u * sig * (1.0 + gp * (1.0 - sig))).astype(bf16)
        du = (dh * act).astype(bf16)
        hd = (act * u).astype(bf16)
        dgate[:, cols] = dg
        dup[:, cols] = du
        for i, (a, b) in enumerate([(xlow_t[:R, :], dg), (xlow_t[R:, :], du), (dylow_t[...], hd)]):
            v = dot(a, b)
            if h == 0:
                pacc[i, :, cols] = v
            else:
                pacc[i, :, cols] += v
        low[:, :R] += dot_nt(dg, a2_ref[0, :, cols])
        low[:, R : 2 * R] += dot_nt(du, a2_ref[1, :, cols])
        low[:, 2 * R :] += dot_nt(hd, df_ref[:, cols])

    def keep_low(h):
        lowb[:, h] = low[...].astype(bf16).reshape(n, S, 3 * R)

    def send_to(src, dst, s_sem, r_sem, peer):
        return pltpu.make_async_remote_copy(
            src_ref=src, dst_ref=dst, send_sem=s_sem, recv_sem=r_sem, device_id=peer, device_id_type=MESH
        )

    def low_copy(k, slot):
        peer = lax.rem(t + k, n)
        return send_to(lowb.at[peer], lowr.at[slot], low_s.at[k], low_r.at[slot], {"tensor": peer})

    def ul_copy(k, slot):
        peer = lax.rem(t + k, n)
        return send_to(ulow.at[slot], ulow.at[slot], ul_s.at[k], ul_r.at[slot], {"tensor": peer})

    def scatter_copy(src, dst, s_sem, r_sem, k, slot):
        peer = lax.rem(d + k, m)
        return send_to(src.at[peer], dst.at[slot], s_sem.at[k], r_sem.at[slot], {"dp": peer})

    def p_copy(k, slot):
        return scatter_copy(psend, precv, p_s, p_r, k, slot)

    def g_copy(k, slot):
        return scatter_copy(gsend, grecv, g_s, g_r, k, slot)

    def pf_copy(k, slot):
        peer = lax.rem(d + k, m)
        return send_to(pfin.at[slot], pfin.at[slot], pf_s.at[k], pf_r.at[slot], {"dp": peer})

    def gf_copy(k, slot):
        peer = lax.rem(d + k, m)
        at = gfin.at[core, slot]
        return send_to(at, at, gf_s.at[k], gf_r.at[slot], {"dp": peer})

    def gd_copy(side, slot):
        at = gfin.at[side, slot]
        return send_to(at, at, gd_s.at[slot], gd_r.at[slot], {"tensor": partner})

    def other_d(k):
        return lax.rem(d + k, m)

    def die_copy(h, c):
        return send_to(term.at[h, c, 1 - core], die.at[h, c], die_s.at[h, c], die_r.at[h, c], {"tensor": partner})

    def rs_copy(h, c, k, slot):
        other = lax.rem(z + k, nz)
        return send_to(
            term.at[h, c, core, other], rsr.at[h, c, slot], rs_s.at[h, c, k], rs_r.at[h, c, slot],
            {"tensor": 2 * other + core},
        )

    def chip_sum(h, c):
        die_copy(h, c).wait_recv()
        term[h, c, core] = (term[h, c, core].astype(f32) + die[h, c].astype(f32)).astype(bf16)
        for k in range(1, nz):
            rs_copy(h, c, k, z).start()

    def term_tile(h, c):
        span = pl.ds(pl.multiple_of(c * W, W), W)
        v = (dot_nt(dgate[...], wg[span, :]) + dot_nt(dup[...], wu[span, :])).astype(bf16)
        v = v.reshape(nz, 2, S, W)
        term[h, c, 0] = v[:, 0]
        term[h, c, 1] = v[:, 1]
        die_copy(h, c).start()

        @pl.when(c > 0)
        def _():
            chip_sum(h, c - 1)

    loads[0].wait()
    start(lines_x[0])
    loop(1, n, lambda s: forward(lines_x[0], s))
    loads[1].wait()
    start(lines_dy[0])
    input_rank(0)
    loads[4].wait()
    loads[5].wait()

    def beside(line, s, h, tile):
        forward(line, s)

        @pl.when(s - 1 < NT)
        def _():
            tile(h, s - 1)

    loop(1, n, lambda s: beside(lines_dy[0], s, 0, forward_tile))
    loop(n - 1, NT, lambda j: forward_tile(0, j))

    loads[2].wait()
    start(lines_x[1])
    cotangent_rank(0)
    loads[6].wait()
    loop(1, n, lambda s: beside(lines_x[1], s, 0, backward_tile))
    loop(n - 1, NT, lambda j: backward_tile(0, j))

    loads[3].wait()
    start(lines_dy[1])
    keep_low(0)
    input_rank(1)
    per = -(-NC // (n - 1))

    def mixed(s):
        forward(lines_dy[1], s)
        for i in range(per):
            c = (s - 1) * per + i

            @pl.when(c < NC)
            def _():
                term_tile(0, c)

        @pl.when(s - 1 < NT)
        def _():
            forward_tile(1, s - 1)

    loop(1, n, mixed)
    loop(n - 1, NT, lambda j: forward_tile(1, j))
    chip_sum(0, NC - 1)

    cotangent_rank(1)
    loop(0, NT, lambda j: backward_tile(1, j))
    keep_low(1)

    loop(1, n, lambda k: low_copy(k, t).start())
    for q in range(m * cp):
        g, j = divmod(q, HC)
        if g < 3:
            psend[q // cp, q % cp] = pacc[g, :, 128 * j : 128 * (j + 1)].astype(bf16)
        else:
            psend[q // cp, q % cp] = jnp.zeros((R, 128), bf16)
    loop(1, m, lambda k: p_copy(k, d).start())

    cut1, cut2, cut3 = NC // 4, NC // 2, (3 * NC) // 4
    loop(0, cut1, lambda c: term_tile(1, c))

    lowr[t] = lowb[t]
    loop(1, n, lambda k: low_copy(k, lax.rem(t + k, n)).wait_recv())
    total = lowr[0].astype(f32)
    for b in range(1, n):
        total = total + lowr[b].astype(f32)
    u_own[...] = total.astype(bf16).reshape(T, 3 * R)
    ulow[t] = total.astype(bf16)
    loop(1, n, lambda k: ul_copy(k, t).start())

    loop(cut1, cut2, lambda c: term_tile(1, c))

    loop(1, n, lambda k: ul_copy(k, lax.rem(t + k, n)).wait_recv())
    u_t = [ulow[:, h].reshape(n * S, 3 * R).astype(f32).T.astype(bf16) for h in range(2)]
    for q in range(2 * m * cg):
        g, j = divmod(q, DC)
        if q % (m * cg) == 0:
            owner_side = q // (m * cg)
        if g < 3:
            src = xg if g < 2 else dyg

            @pl.when(core == owner_side)
            def _(q=q, g=g, j=j, src=src):
                acc = 0.0
                for h in range(2):
                    acc = acc + dot(u_t[h][g * R : (g + 1) * R], src[h, :, 128 * j : 128 * (j + 1)])
                gsend[(q // cg) % m, q % cg] = acc.astype(bf16)
        else:

            @pl.when(core == owner_side)
            def _(q=q):
                gsend[(q // cg) % m, q % cg] = jnp.zeros((R, 128), bf16)

    loop(1, m, lambda k: g_copy(k, d).start())

    loop(cut2, cut3, lambda c: term_tile(1, c))

    precv[d] = psend[d]
    loop(1, m, lambda k: p_copy(k, other_d(k)).wait_recv())
    total = precv[0].astype(f32)
    for e in range(1, m):
        total = total + precv[e].astype(f32)
    pfin[d] = total.astype(bf16)
    loop(1, m, lambda k: pf_copy(k, d).start())

    loop(cut3, NC, lambda c: term_tile(1, c))
    chip_sum(1, NC - 1)

    grecv[d] = gsend[d]
    loop(1, m, lambda k: g_copy(k, other_d(k)).wait_recv())
    total = grecv[0].astype(f32)
    for e in range(1, m):
        total = total + grecv[e].astype(f32)
    gfin[core, d] = total.astype(bf16)
    loop(1, m, lambda k: gf_copy(k, d).start())
    gd_copy(core, d).start()

    loop(1, m, lambda k: pf_copy(k, other_d(k)).wait_recv())
    for q in range(3 * HC):
        g, j = divmod(q, HC)
        v = pfin[q // cp, q % cp].astype(f32)
        if g < 2:
            p2_ref[g, :, 128 * j : 128 * (j + 1)] = v
        else:
            p1_ref[:, 128 * j : 128 * (j + 1)] = v

    def finish(h, c):
        span = pl.ds(pl.multiple_of(c * W, W), W)
        part = slice(h * S, (h + 1) * S)
        total = term[h, c, core, z].astype(f32) + adapter_scale * dot_nt(u_own[part, : 2 * R], a1_ref[span, :])
        for k in range(1, nz):
            other = lax.rem(z + k, nz)
            rs_copy(h, c, k, other).wait_recv()
            total = total + rsr[h, c, other].astype(f32)
        ig_ref[part, span] = total.astype(bf16)

    loop(0, NC, lambda c: finish(0, c))

    def pass_on(k):
        gf_copy(k, other_d(k)).wait_recv()
        gd_copy(core, other_d(k)).start()

    loop(1, m, pass_on)
    loop(0, m, lambda e: gd_copy(1 - core, e).wait_recv())

    def g_chunk(g, j):
        q = g * DC + j
        return gfin[q // (m * cg), (q // cg) % m, q % cg].astype(f32)

    for j in range(DC):
        both = jnp.concatenate([g_chunk(0, j), g_chunk(1, j)], axis=0)
        first_ref[128 * j : 128 * (j + 1), :] = both.T
        second_ref[:, 128 * j : 128 * (j + 1)] = g_chunk(2, j)

    loop(0, NC, lambda c: finish(1, c))

    for line in lines_x + lines_dy:
        drain(line)
    loop(1, n, lambda k: low_copy(k, t).wait_send())
    loop(1, n, lambda k: ul_copy(k, t).wait_send())
    loop(1, m, lambda k: p_copy(k, d).wait_send())
    loop(1, m, lambda k: pf_copy(k, d).wait_send())
    loop(1, m, lambda k: g_copy(k, d).wait_send())
    loop(1, m, lambda k: gf_copy(k, d).wait_send())
    loop(0, m, lambda e: gd_copy(core, e).wait_send())

    def sent(c):
        for h in range(2):
            die_copy(h, c).wait_send()
            for k in range(1, nz):
                rs_copy(h, c, k, z).wait_send()

    loop(0, NC, sent)


def shards(x, dy, wg, wu, wd, a1, a2, df, d2):
    n = lax.axis_size("tensor")
    m = lax.axis_size("dp")
    T, D = x.shape
    H = wg.shape[1]
    R = a2.shape[1]
    S = T // 2
    GH = n * S
    TW = 256 if H % 256 == 0 else 128
    W = 256
    NC = D // W
    cp = -(-3 * (H // 128) // m)
    cg = -(-3 * (D // 128) // (2 * m))
    factor = adapter_scale / math.sqrt(T * n * m)
    nz = n // 2
    V = pltpu.VMEM
    DMA = pltpu.SemaphoreType.DMA
    any_spec = pl.BlockSpec(memory_space=pl.ANY)
    vmem_spec = pl.BlockSpec(memory_space=pltpu.VMEM)
    macs = 5 * n * T * D * H
    ig, first, second, p2, p1 = pl.pallas_call(
        functools.partial(kernel, n, m, T, H, R, TW, W, cp, cg),
        out_shape=(
            jax.ShapeDtypeStruct((T, D), bf16),
            jax.ShapeDtypeStruct((D, 2 * R), f32),
            jax.ShapeDtypeStruct((R, D), f32),
            jax.ShapeDtypeStruct((2, R, H), f32),
            jax.ShapeDtypeStruct((R, H), f32),
        ),
        in_specs=[any_spec] * 5 + [vmem_spec] * 4,
        out_specs=(vmem_spec,) * 5,
        scratch_shapes=[
            V((2, GH, D), bf16), V((2, GH, D), bf16),
            V((D, H), bf16), V((D, H), bf16), V((H, D), bf16),
            V((GH, H), f32), V((GH, H), f32), V((GH, H), bf16), V((GH, H), bf16),
            V((GH, 2 * R), bf16), V((2 * R, GH), bf16), V((GH, R), bf16), V((R, GH), bf16),
            V((GH, 3 * R), f32), V((n, 2, S, 3 * R), bf16), V((n, 2, S, 3 * R), bf16),
            V((n, 2, S, 3 * R), bf16), V((T, 3 * R), bf16),
            V((3, R, H), f32), V((m, cp, R, 128), bf16), V((m, cp, R, 128), bf16), V((m, cp, R, 128), bf16),
            V((m, cg, R, 128), bf16), V((m, cg, R, 128), bf16), V((2, m, cg, R, 128), bf16),
            V((2, NC, 2, nz, S, W), bf16), V((2, NC, nz, S, W), bf16), V((2, NC, nz, S, W), bf16),
            DMA((7,)),
            DMA((2, 3, n)), DMA((2, n)), DMA((2, 3, n)), DMA((2, n)),
            DMA((n,)), DMA((n,)), DMA((n,)), DMA((n,)),
            DMA((m,)), DMA((m,)), DMA((m,)), DMA((m,)),
            DMA((m,)), DMA((m,)), DMA((m,)), DMA((m,)), DMA((m,)), DMA((m,)),
            DMA((2, NC)), DMA((2, NC)), DMA((2, NC, nz)), DMA((2, NC, nz)),
        ],
        compiler_params=pltpu.CompilerParams(
            collective_id=0, has_side_effects=True, vmem_limit_bytes=63 * 1024 * 1024
        ),
        cost_estimate=pl.CostEstimate(flops=2 * macs, bytes_accessed=6 * D * H, transcendentals=n * T * H),
    )(x, dy, wg, wu, wd, a1, a2, df, d2)
    return ig, factor * first, factor * p2, factor * p1, factor * second


def solution(mesh):
    in_specs = (
        P(("dp", "tensor"), None),
        P(("dp", "tensor"), None),
        P(None, "tensor"),
        P(None, "tensor"),
        P("tensor", None),
        P(),
        P(None, None, "tensor"),
        P(None, "tensor"),
        P(),
    )
    out_specs = (P(("dp", "tensor"), None), P(), P(None, None, "tensor"), P(None, "tensor"), P())
    return jax.shard_map(shards, mesh=mesh, in_specs=in_specs, out_specs=out_specs, check_vma=False)
```
